32 devices in a mesh: height: 4 (over x, core), width: 4 (over z), head: 2 (over y).
Axes of the slice: x: 2, y: 2, z: 4, core: 2. Of those that a mesh axis runs over, the one named last changes fastest.
Arguments:
- tokens: bfloat16 [4, 8, 144, 1536], P('height', 'width'), may hold values from -6 to 6
- grad_out: bfloat16 [4, 8, 144, 1536], P('height', 'width'), may hold values from -6 to 6
- qkv_weight: bfloat16 [1536, 3, 768], P(('height', 'width'), None, 'head'), may hold values from -0.15625 to 0.15625
- out_weight: bfloat16 [1536, 768], P(('height', 'width'), 'head'), may hold values from -0.5 to 0.5
- q_gain: float32 [768], P('head'), may hold values from 0.5 to 2
- k_gain: float32 [768], P('head'), may hold values from 0.5 to 2
- key_valid: int32 [4, 8, 144], P('height', 'width'), may hold values from 0 to 1, as said below
Outputs:
- mixed: bfloat16 [4, 8, 144, 1536], P('height', 'width', None, 'head')
- grad_in: bfloat16 [4, 8, 144, 1536], P('height', 'width', None, 'head')
The draws below stay inside these ranges and needn't reach their ends.
Inputs may be any that keep to these rules, and one draw needn't show every extreme that they name: key_valid is 0 only in the last row of tiles and in the last column of tiles. In a tile of the last row, each frame and column within the tile has its own count of valid rows, 1 to 5, and the rows from that count on are 0. In a tile of the last column, each frame and row within the tile has its own count of valid columns, 1 to 8, and the columns from that count on are 0. The first token of every tile is valid.
All inputs are finite; a program needn't handle non-finite values.
Results may differ from the reference program's by a relative error of at most 0.015.
Values may be sent and summed in bfloat16 or wider, within the bound.
A program may use at most 128 MiB of HBM per device.

```python
import math
import jax
import jax.numpy as jnp
from jax import lax

D = 1536
HEAD_DIM = 128
HEADS = 6
FRAMES = 3
TILE_ROWS = 6
TILE_COLS = 8
TILE_TOK = 144
TILES_H = 4
TILES_W = 8
N_HEAD = 2


def draw_key_valid(key, part):
    key = jax.random.fold_in(key, 11)
    row_key, col_key = jax.random.split(key)
    row_counts = jax.random.randint(row_key, (TILES_W, FRAMES, TILE_COLS), 1, TILE_ROWS)
    col_counts = jax.random.randint(col_key, (TILES_H, FRAMES, TILE_ROWS), 1, TILE_COLS + 1)
    within = jnp.arange(TILE_TOK)
    frame_index = within // (TILE_ROWS * TILE_COLS)
    grid_row = within // TILE_COLS % TILE_ROWS
    grid_col = within % TILE_COLS
    row_limit = row_counts[:, frame_index, grid_col].reshape(1, TILES_W, TILE_TOK)
    col_limit = col_counts[:, frame_index, grid_row].reshape(TILES_H, 1, TILE_TOK)
    tile_row = jnp.arange(TILES_H).reshape(-1, 1, 1)
    tile_col = jnp.arange(TILES_W).reshape(1, -1, 1)
    row_pad = (tile_row == TILES_H - 1) & (grid_row.reshape(1, 1, -1) >= row_limit)
    col_pad = (tile_col == TILES_W - 1) & (grid_col.reshape(1, 1, -1) >= col_limit)
    return jnp.where(row_pad | col_pad, 0, 1).astype(jnp.int32)


def block_scale(own_key, extent, pieces, low, high):
    def one(axis_at, blocks):
        heights = jax.random.uniform(jax.random.fold_in(jax.random.fold_in(own_key, 6), axis_at), (blocks,), jnp.float32, low / len(pieces), high / len(pieces))
        return jnp.repeat(jnp.exp(heights), extent[axis_at] // blocks).reshape((-1,) + (1,) * (len(extent) - axis_at - 1))

    level = one(*pieces[0])
    for cut in pieces[1:]:
        level = level * one(*cut)
    return level


def centred(key, dims, deviation, reach, shards=(), dtype=jnp.bfloat16):
    entries = jax.random.normal(key, dims, jnp.float32) * deviation
    if len(shards) > 0:
        entries = block_scale(key, dims, shards, -0.22, 0.18) * entries
    return jnp.clip(entries, min=-reach, max=reach).astype(dtype)


def setup_inputs(seed: int = 0) -> dict:
    keys = jax.random.split(jax.random.key(seed), 8)
    tokens = centred(keys[0], (TILES_H, TILES_W, TILE_TOK, D), 1.0, 6.0, ((0, 4), (1, 4)))
    grad_out = centred(keys[1], (TILES_H, TILES_W, TILE_TOK, D), 1.0, 6.0, ((0, 4), (1, 4)))
    qkv_weight = centred(keys[2], (D, 3, HEADS * HEAD_DIM), D ** -0.5, 0.15625, ((0, 16), (2, 2)))
    out_weight = centred(keys[3], (D, HEADS * HEAD_DIM), HEAD_DIM ** -0.5, 0.5, ((0, 16), (1, 2)))
    q_gain = jnp.clip(jnp.exp(math.log(2.0) - 1.3862944 * jax.random.uniform(keys[4], (HEADS * HEAD_DIM,), jnp.float32) ** block_scale(keys[4], (HEADS * HEAD_DIM,), ((0, 2),), -0.2, 0.2)), 0.5, 2.0)
    k_gain = jnp.clip(jnp.exp(math.log(2.0) - 1.3862944 * jax.random.uniform(keys[5], (HEADS * HEAD_DIM,), jnp.float32) ** block_scale(keys[5], (HEADS * HEAD_DIM,), ((0, 2),), -0.2, 0.2)), 0.5, 2.0)
    key_valid = draw_key_valid(jax.random.fold_in(keys[7], 71), 0)
    return {"tokens": tokens, "grad_out": grad_out, "qkv_weight": qkv_weight, "out_weight": out_weight, "q_gain": q_gain, "k_gain": k_gain, "key_valid": key_valid}


epsilon = 1e-06

def norm_scale(raw_values, gain_vec):
    inverse = lax.rsqrt(lax.optimization_barrier(jnp.mean(raw_values * raw_values, axis=-1, keepdims=True)) + epsilon)
    return (raw_values * inverse * gain_vec, inverse)

def norm_backward(raw_values, inverse, gain_vec, upstream):
    weighted = gain_vec * upstream
    inner_mean = lax.optimization_barrier(jnp.mean(weighted * raw_values, axis=-1, keepdims=True))
    return inverse * weighted - raw_values * inverse ** 3 * inner_mean

def windows(extended, tile_rows, tile_cols):
    return jnp.stack([extended[row_step:row_step + tile_rows, col_step:col_step + tile_cols] for row_step in range(3) for col_step in range(3)], axis=2)

def fold_windows(windowed, tile_rows, tile_cols):
    total = jnp.zeros((tile_rows + 2, tile_cols + 2) + windowed.shape[3:], jnp.float32)
    for position in range(9):
        row_step, col_step = divmod(position, 3)
        total = total.at[row_step:row_step + tile_rows, col_step:col_step + tile_cols].add(windowed[:, :, position])
    return total

def attend(queries, win_keys, win_values, win_valid, upstream):
    factor = HEAD_DIM ** (-0.5)
    query_f = queries.astype(jnp.float32)
    keys_f = win_keys.astype(jnp.float32)
    values_f = win_values.astype(jnp.float32)
    upstream_f = upstream.astype(jnp.float32)
    scores = jnp.einsum('bqhe,bkhe->bhqk', query_f, keys_f) * factor
    weights = jnp.exp(scores) * win_valid[:, None, None, :]
    attn_probs = weights / lax.optimization_barrier(jnp.sum(weights, axis=-1, keepdims=True))
    attn_weights = attn_probs.astype(jnp.bfloat16).astype(jnp.float32)
    attended = jnp.einsum('bhqk,bkhe->bqhe', attn_weights, values_f).astype(jnp.bfloat16)
    grad_probs = jnp.einsum('bqhe,bkhe->bhqk', upstream_f, values_f)
    grad_scores = attn_probs * (grad_probs - lax.optimization_barrier(jnp.sum(attn_probs * grad_probs, axis=-1, keepdims=True)))
    grad_scores = grad_scores.astype(jnp.bfloat16).astype(jnp.float32)
    grad_values = jnp.einsum('bhqk,bqhe->bkhe', attn_weights, upstream_f)
    grad_keys = jnp.einsum('bhqk,bqhe->bkhe', grad_scores, query_f) * factor
    grad_queries = jnp.einsum('bhqk,bkhe->bqhe', grad_scores, keys_f) * factor
    return (attended, grad_queries, grad_keys, grad_values)

def rounded(values):
    return lax.optimization_barrier(values.astype(jnp.bfloat16)).astype(jnp.float32)

def group_sum(left, right, group_count, inner_width):
    total = jnp.zeros((left.shape[0], right.shape[0]), jnp.float32)
    for group_index in range(group_count):
        left_part = left[:, :, group_index * inner_width:(group_index + 1) * inner_width].reshape(left.shape[0], -1)
        right_part = right[:, :, group_index * inner_width:(group_index + 1) * inner_width].reshape(right.shape[0], -1)
        total = total + rounded(jnp.dot(left_part, right_part.T, preferred_element_type=jnp.float32))
    return total.astype(jnp.bfloat16)

def reference(tokens, grad_out, qkv_weight, out_weight, q_gain, k_gain, key_valid):
    head_count = q_gain.shape[0] // HEAD_DIM
    all_inner = head_count * HEAD_DIM
    token_rows = tokens.reshape(-1, D)
    token_count = token_rows.shape[0]
    projected = jnp.dot(token_rows, qkv_weight.reshape(D, 3 * all_inner), preferred_element_type=jnp.float32)
    projected = projected.reshape(token_count, 3, head_count, HEAD_DIM)
    q_raw = projected[:, 0]
    k_raw = projected[:, 1]
    v_raw = projected[:, 2]
    q_gains = q_gain.reshape(head_count, HEAD_DIM)
    k_gains = k_gain.reshape(head_count, HEAD_DIM)
    q_normed, q_inverse = norm_scale(q_raw, q_gains)
    k_normed, k_inverse = norm_scale(k_raw, k_gains)
    shape_tiles = (TILES_H, TILES_W, TILE_TOK, head_count, HEAD_DIM)
    queries = q_normed.astype(jnp.bfloat16).reshape(shape_tiles)
    keys_tiled = k_normed.astype(jnp.bfloat16).reshape(shape_tiles)
    values_tiled = v_raw.astype(jnp.bfloat16).reshape(shape_tiles)
    border = ((1, 1), (1, 1), (0, 0), (0, 0), (0, 0))
    win_keys = windows(jnp.pad(keys_tiled, border), TILES_H, TILES_W).reshape(TILES_H, TILES_W, 9 * TILE_TOK, head_count, HEAD_DIM)
    win_values = windows(jnp.pad(values_tiled, border), TILES_H, TILES_W).reshape(TILES_H, TILES_W, 9 * TILE_TOK, head_count, HEAD_DIM)
    valid_ext = jnp.pad(key_valid.astype(jnp.float32), ((1, 1), (1, 1), (0, 0)))
    win_valid = windows(valid_ext, TILES_H, TILES_W).reshape(TILES_H, TILES_W, 9 * TILE_TOK)
    grad_attended = jnp.dot(grad_out.reshape(-1, D), out_weight, preferred_element_type=jnp.float32)
    grad_attended = grad_attended.astype(jnp.bfloat16).reshape(shape_tiles)

    def one_row(items):
        return attend(*items)
    attended, grad_queries, grad_keys_win, grad_values_win = lax.map(one_row, (queries, win_keys, win_values, win_valid, grad_attended))
    win_shape = (TILES_H, TILES_W, 9, TILE_TOK, head_count, HEAD_DIM)
    grad_keys = fold_windows(grad_keys_win.reshape(win_shape), TILES_H, TILES_W)[1:-1, 1:-1]
    grad_values = fold_windows(grad_values_win.reshape(win_shape), TILES_H, TILES_W)[1:-1, 1:-1]
    grad_q_raw = norm_backward(q_raw, q_inverse, q_gains, grad_queries.reshape(token_count, head_count, HEAD_DIM))
    grad_k_raw = norm_backward(k_raw, k_inverse, k_gains, grad_keys.reshape(token_count, head_count, HEAD_DIM))
    grad_qkv = jnp.stack([grad_q_raw, grad_k_raw, grad_values.reshape(token_count, head_count, HEAD_DIM)], axis=1)
    grad_qkv = grad_qkv.reshape(token_count, 3, all_inner).astype(jnp.bfloat16)
    inner_width = all_inner // N_HEAD
    mixed = group_sum(attended.reshape(token_count, 1, all_inner), out_weight.reshape(D, 1, all_inner), N_HEAD, inner_width)
    grad_in = group_sum(grad_qkv, qkv_weight, N_HEAD, inner_width)
    out_shape = (TILES_H, TILES_W, TILE_TOK, D)
    return (mixed.reshape(out_shape), grad_in.reshape(out_shape))
```

```python
import functools

import jax
import jax.numpy as jnp
from jax import lax
from jax.experimental import pallas as pl
from jax.experimental.pallas import tpu as pltpu
from jax.sharding import PartitionSpec as P

HEAD_DIM = 128
EPS = 1e-06
FACTOR = HEAD_DIM**-0.5
LOG2E = 1.4426950408889634
ABSENT = 1e30
NT = (((1,), (1,)), ((), ()))
TN = (((0,), (0,)), ((), ()))
F32 = jnp.float32
BF16 = jnp.bfloat16


def mm(a, b, dims=(((1,), (0,)), ((), ()))):
    return lax.dot_general(a, b, dims, preferred_element_type=F32)


def body(cfg, *refs):
    nh, nw, heads, tt, gather = cfg
    tok, go, win, qg, kg, vcol, mixed, gin = refs[:8]
    rest = list(refs[8:])
    W = rest.pop(0) if gather else win
    (raw, ga, qb, kv, kc, gacc, att, gq, gs, gr, gs2, gr2, gqkv, ms, mr, ss, sr) = rest[:17]
    (s_h, r_h, s_g, r_g, s_y, r_y) = rest[17:23]
    width = heads * HEAD_DIM
    h, w, y = lax.axis_index("height"), lax.axis_index("width"), lax.axis_index("head")
    up, down, left, right = h > 0, h < nh - 1, w > 0, w < nw - 1
    peer = (h, w, 1 - y)
    dev = {"u": (h - 1, w, y), "d": (h + 1, w, y), "l": (h, w - 1, y), "r": (h, w + 1, y)}
    there = {"u": up, "d": down, "l": left, "r": right}
    xdev = (lax.rem(h + 2, nh), w, y)
    cdev = (h + 1 - 2 * lax.rem(h, 2), w, y)

    def copy(src, dst, ssem, rsem, to):
        return pltpu.make_async_remote_copy(
            src_ref=src, dst_ref=dst, send_sem=ssem, recv_sem=rsem,
            device_id=to, device_id_type=pl.DeviceIdType.MESH)

    barrier = pltpu.get_barrier_semaphore()

    def greet(to):
        pl.semaphore_signal(barrier, inc=1, device_id=to, device_id_type=pl.DeviceIdType.MESH)

    count = 1
    for side in "udlr":
        pl.when(there[side])(functools.partial(greet, dev[side]))
        count = count + there[side].astype(jnp.int32)
    greet(peer)
    if gather:
        greet(xdev)
        greet(cdev)
        count = count + 2
    pl.semaphore_wait(barrier, count)

    if gather:
        s_z, r_z, s_x, r_x, s_c, r_c = rest[23:29]
        rows = win.shape[0]
        total = 2 * nw - 1

        def shard(hh, ww):
            return W.at[pl.ds(pl.multiple_of((hh * nw + ww) * rows, 16), rows), :]

        def column(i):
            if i == 0:
                return w
            k, d = divmod(i - 1, 2)
            return w + 1 + k if d else w - 1 - k

        def held(i):
            if i == 0:
                return w >= 0
            return column(i) < nw if (i - 1) % 2 else column(i) >= 0

        def zc(d, k):
            part = shard(h, w + k if d else w - k)
            return copy(part, part, s_z.at[d, k], r_z.at[d, k], dev["l" if d else "r"])

        def xc(i):
            part = shard(h, column(i))
            return copy(part, part, s_x.at[i], r_x.at[i], xdev)

        def cc(i):
            part = shard(h, column(i)) if i < total else shard(xdev[0], column(i - total))
            return copy(part, part, s_c.at[i], r_c.at[i], cdev)

        W[pl.ds(pl.multiple_of((h * nw + w) * rows, 16), rows), :] = win[...]
        pl.when(right)(lambda: zc(0, 0).start())
        pl.when(left)(lambda: zc(1, 0).start())
        xc(0).start()
        cc(0).start()

    def fill(index):
        shape = kv.at[index].shape[:-1] + (HEAD_DIM,)
        kv[index + (slice(0, HEAD_DIM),)] = jnp.full(shape, ABSENT, BF16)
        kv[index + (slice(HEAD_DIM, 2 * HEAD_DIM),)] = jnp.zeros(shape, BF16)

    every = slice(None)
    for hd in range(heads):
        for c in range(4):
            pl.when(jnp.logical_not(up))(functools.partial(fill, (hd, c, 0, every)))
            pl.when(jnp.logical_not(down))(functools.partial(fill, (hd, c, 2, every)))
        pl.when(jnp.logical_not(left) & up)(functools.partial(fill, (hd, 0, 0, every)))
        pl.when(jnp.logical_not(right) & up)(functools.partial(fill, (hd, 3, 0, every)))
        pl.when(jnp.logical_not(left) & down)(functools.partial(fill, (hd, 0, 2, every)))
        pl.when(jnp.logical_not(right) & down)(functools.partial(fill, (hd, 3, 2, every)))
        pl.when(jnp.logical_not(left))(functools.partial(fill, (hd, 0, 1, every)))
        pl.when(jnp.logical_not(right))(functools.partial(fill, (hd, 3, 1, every)))

    if gather:
        def pass_x(i):
            xc(i).wait_recv()
            cc(total + i).start()

        def step(d, k):
            zc(d, k).wait_recv()
            if k + 1 < nw - 1:
                pl.when(left if d else right)(lambda: zc(d, k + 1).start())
            xc(1 + 2 * k + d).start()
            cc(1 + 2 * k + d).start()

        for k in range(nw - 1):
            for d in range(2):
                pl.when(held(1 + 2 * k + d))(functools.partial(step, d, k))
            for i in ([0] if k == 0 else [2 * k - 1, 2 * k]):
                pl.when(held(i))(functools.partial(pass_x, i))
        for i in (2 * nw - 3, 2 * nw - 2):
            pl.when(held(i))(functools.partial(pass_x, i))
        for i in range(total):
            def done(i=i):
                xc(i).wait_send()
                for j in (i, total + i):
                    cc(j).wait_recv()
                    cc(j).wait_send()
            pl.when(held(i))(done)
        for k in range(nw - 1):
            pl.when(right & (w - k >= 0))(lambda: zc(0, k).wait_send())
            pl.when(left & (w + k < nw))(lambda: zc(1, k).wait_send())

    def tile(hd, c, r):
        return kv.at[hd, c, r]

    def side_copy(hd, side):
        if side == "l":
            return copy(tile(hd, 1, 1), tile(hd, 3, 1), s_h.at[hd, 0], r_h.at[hd, 0], dev["l"])
        if side == "r":
            return copy(tile(hd, 2, 1), tile(hd, 0, 1), s_h.at[hd, 1], r_h.at[hd, 1], dev["r"])
        at, i = (2, 2) if side == "u" else (0, 3)
        return copy(kv.at[hd, pl.ds(1, 2), 1], kv.at[hd, pl.ds(1, 2), at],
                    s_h.at[hd, i], r_h.at[hd, i], dev[side])

    def corner(hd, side, c):
        at, i = (2, 4) if side == "u" else (0, 6)
        i += c // 3
        return copy(tile(hd, c, 1), tile(hd, c, at), s_h.at[hd, i], r_h.at[hd, i], dev[side])

    raw[:, width:] = mm(tok[...], W[:, width : 3 * width])
    absent = vcol[...] == 0
    for hd in range(heads):
        cols = slice(hd * HEAD_DIM, (hd + 1) * HEAD_DIM)
        k_raw = raw[:, width + hd * HEAD_DIM : width + (hd + 1) * HEAD_DIM]
        inv = lax.rsqrt(jnp.mean(k_raw * k_raw, axis=-1, keepdims=True) + EPS)
        kn = jnp.where(absent, ABSENT, k_raw * inv * kg[:, cols]).astype(BF16)
        v = raw[:, 2 * width + hd * HEAD_DIM : 2 * width + (hd + 1) * HEAD_DIM].astype(BF16)
        for j in range(2):
            kv[hd, 1 + j, 1, :, 0:HEAD_DIM] = kn[j * tt : (j + 1) * tt]
            kv[hd, 1 + j, 1, :, HEAD_DIM:] = v[j * tt : (j + 1) * tt]
        for side in "lrud":
            pl.when(there[side])(lambda: side_copy(hd, side).start())

    raw[:, 0:width] = mm(tok[...], W[:, 0:width])
    ga[...] = mm(go[...], W[:, 3 * width : 4 * width]).astype(BF16)
    for hd in range(heads):
        cols = slice(hd * HEAD_DIM, (hd + 1) * HEAD_DIM)
        q_raw = raw[:, cols]
        inv = lax.rsqrt(jnp.mean(q_raw * q_raw, axis=-1, keepdims=True) + EPS)
        qb[:, cols] = (q_raw * inv * qg[:, cols]).astype(BF16)

    def forward(hd, side, c):
        side_copy(hd, "r" if c == 0 else "l").wait_recv()
        for s in "ud":
            pl.when(there[s])(lambda: corner(hd, s, c).start())

    for hd in range(heads):
        pl.when(left)(functools.partial(forward, hd, "l", 0))
        pl.when(right)(functools.partial(forward, hd, "r", 3))

    def back(hd, side):
        i = 0 if side == "u" else 1
        return copy(gs.at[hd, i], gr.at[hd, i], s_g.at[hd, i], r_g.at[hd, i], dev[side])

    def back2(hd, side):
        i = 0 if side == "l" else 1
        return copy(gs2.at[hd, i], gr2.at[hd, i], s_g.at[hd, 2 + i], r_g.at[hd, 2 + i], dev[side])

    win_rows = 9 * tt
    for hd in range(heads):
        cols = slice(hd * HEAD_DIM, (hd + 1) * HEAD_DIM)
        for side, other in (("d", "u"), ("u", "d")):
            def arrived(side=side, other=other):
                side_copy(hd, other).wait_recv()
                pl.when(left)(lambda: corner(hd, other, 0).wait_recv())
                pl.when(right)(lambda: corner(hd, other, 3).wait_recv())
            pl.when(there[side])(arrived)
        keys = kv[hd, :, :, :, 0:HEAD_DIM].reshape(12 * tt, HEAD_DIM).astype(F32)
        out = keys > ABSENT * 0.1
        kc[:, 0:HEAD_DIM] = jnp.where(out, 0.0, keys).astype(BF16)
        kc[:, HEAD_DIM:] = jnp.where(out, -1e9, 0.0).astype(BF16)
        for j in range(2):
            rows_j = slice(j * tt, (j + 1) * tt)
            span = slice(3 * j * tt, 3 * j * tt + win_rows)
            q = qb[rows_j, cols]
            up_ = ga[rows_j, cols]
            both = kc[span, :]
            values = kv[hd, j : j + 3, :, :, HEAD_DIM:].reshape(win_rows, HEAD_DIM)
            s = mm(jnp.concatenate([q, jnp.ones_like(q)], axis=1), both, NT)
            e = jnp.exp2(s * (FACTOR * LOG2E))
            p = e * (1.0 / jnp.sum(e, axis=-1, keepdims=True))
            pb = p.astype(BF16)
            att[rows_j, cols] = mm(pb, values).astype(BF16)
            gp = mm(up_, values, NT)
            ds = (p * (gp - jnp.sum(p * gp, axis=-1, keepdims=True))).astype(BF16)
            gq[rows_j, cols] = mm(ds, both[:, 0:HEAD_DIM]) * FACTOR
            dk = mm(ds, q, TN) * FACTOR
            dv = mm(pb, up_, TN)
            if j == 0:
                gacc[hd, 0:win_rows, 0:HEAD_DIM] = dk
                gacc[hd, 0:win_rows, HEAD_DIM:] = dv
            else:
                lo = 3 * tt
                gacc[hd, lo:win_rows, 0:HEAD_DIM] += dk[: win_rows - lo]
                gacc[hd, lo:win_rows, HEAD_DIM:] += dv[: win_rows - lo]
                gacc[hd, win_rows:, 0:HEAD_DIM] = dk[win_rows - lo :]
                gacc[hd, win_rows:, HEAD_DIM:] = dv[win_rows - lo :]
        for i, side in ((0, "u"), (1, "d")):
            for c in range(4):
                at = (3 * c + 2 * i) * tt
                gs[hd, i, c] = gacc[hd, at : at + tt, :].astype(BF16)
            pl.when(there[side])(lambda: back(hd, side).start())

    half = gin.shape[1]
    other_rows = pl.ds(pl.multiple_of((1 - y) * half, 128), half)
    own_rows = pl.ds(pl.multiple_of(y * half, 128), half)
    m_copy = copy(ms, mr, s_y.at[0], r_y.at[0], peer)
    ms[...] = mm(att[...], W[other_rows, 3 * width : 4 * width], NT).astype(BF16)
    m_copy.start()

    def norm_back(x, gain, g):
        inv = lax.rsqrt(jnp.mean(x * x, axis=-1, keepdims=True) + EPS)
        wg = gain * g
        inner = jnp.mean(wg * x, axis=-1, keepdims=True)
        return (inv * wg - x * (inv * inv * inv) * inner).astype(BF16)

    for hd in range(heads):
        for i, (side, other) in enumerate((("u", "d"), ("d", "u"))):
            def add(i=i, side=side, other=other):
                back(hd, other).wait_recv()
                for c in range(4):
                    at = (3 * c + 1) * tt
                    gacc[hd, at : at + tt, :] += gr[hd, 1 - i, c].astype(F32)
            pl.when(there[side])(add)
        for i, (side, c) in enumerate((("l", 0), ("r", 3))):
            def send(i=i, side=side, c=c):
                at = (3 * c + 1) * tt
                gs2[hd, i] = gacc[hd, at : at + tt, :].astype(BF16)
                back2(hd, side).start()
            pl.when(there[side])(send)

    own_mixed = mm(att[...], W[own_rows, 3 * width : 4 * width], NT).astype(BF16).astype(F32)
    for hd in range(heads):
        cols = slice(hd * HEAD_DIM, (hd + 1) * HEAD_DIM)
        gqkv[:, cols] = norm_back(raw[:, cols], qg[:, cols], gq[:, cols])
    m_copy.wait_recv()
    mixed[...] = (own_mixed + mr[...].astype(F32)).astype(BF16)

    for hd in range(heads):
        for i, (side, other, c) in enumerate((("l", "r", 1), ("r", "l", 2))):
            def add2(i=i, other=other, c=c):
                back2(hd, other).wait_recv()
                at = (3 * c + 1) * tt
                gacc[hd, at : at + tt, :] += gr2[hd, 1 - i].astype(F32)
            pl.when(there[side])(add2)
        cols = slice(hd * HEAD_DIM, (hd + 1) * HEAD_DIM)
        kcols = slice(width + hd * HEAD_DIM, width + (hd + 1) * HEAD_DIM)
        vcols = slice(2 * width + hd * HEAD_DIM, 2 * width + (hd + 1) * HEAD_DIM)
        for j in range(2):
            rows_j = slice(j * tt, (j + 1) * tt)
            at = (3 * (1 + j) + 1) * tt
            gqkv[rows_j, kcols] = norm_back(
                raw[rows_j, kcols], kg[:, cols], gacc[hd, at : at + tt, 0:HEAD_DIM])
            gqkv[rows_j, vcols] = gacc[hd, at : at + tt, HEAD_DIM:].astype(BF16)

    def in_copy(j):
        return copy(ss.at[j], sr.at[j], s_y.at[1 + j], r_y.at[1 + j], peer)

    for j in range(2):
        rows_j = slice(j * tt, (j + 1) * tt)
        ss[j] = mm(gqkv[rows_j, :], W[other_rows, 0 : 3 * width], NT).astype(BF16)
        in_copy(j).start()
    own_in = mm(gqkv[...], W[own_rows, 0 : 3 * width], NT).astype(BF16).astype(F32)
    for j in range(2):
        rows_j = slice(j * tt, (j + 1) * tt)
        in_copy(j).wait_recv()
        gin[rows_j, :] = (own_in[rows_j] + sr[j].astype(F32)).astype(BF16)

    m_copy.wait_send()
    for j in range(2):
        in_copy(j).wait_send()
    for hd in range(heads):
        for side in "lrud":
            pl.when(there[side])(lambda: side_copy(hd, side).wait_send())
        for s in "ud":
            pl.when(there[s] & left)(lambda: corner(hd, s, 0).wait_send())
            pl.when(there[s] & right)(lambda: corner(hd, s, 3).wait_send())
            pl.when(there[s])(lambda: back(hd, s).wait_send())
        for s in "lr":
            pl.when(there[s])(lambda: back2(hd, s).wait_send())


def on_device(nh, nw, tokens, grad_out, qkv_weight, out_weight, q_gain, k_gain, key_valid):
    tile_rows, tile_cols, tt, model = tokens.shape
    count = tile_rows * tile_cols * tt
    width = q_gain.shape[0]
    heads = width // HEAD_DIM
    weights = jnp.concatenate(
        [qkv_weight.reshape(qkv_weight.shape[0], 3 * width), out_weight], axis=1)
    gather = nh == 4 and nw > 1 and weights.shape[0] % 16 == 0
    if not gather:
        weights = lax.all_gather(weights, ("height", "width"), axis=0, tiled=True)
    vcol = jnp.broadcast_to(key_valid.astype(F32).reshape(count, 1), (count, HEAD_DIM))
    half = model // 2
    vm = pltpu.VMEM
    dma = pltpu.SemaphoreType.DMA
    scratch = [vm((model, 4 * width), BF16)] if gather else []
    scratch += [
        vm((count, 3 * width), F32),
        vm((count, width), BF16),
        vm((count, width), BF16),
        vm((heads, 4, 3, tt, 2 * HEAD_DIM), BF16),
        vm((12 * tt, 2 * HEAD_DIM), BF16),
        vm((heads, 12 * tt, 2 * HEAD_DIM), F32),
        vm((count, width), BF16),
        vm((count, width), F32),
        vm((heads, 2, 4, tt, 2 * HEAD_DIM), BF16),
        vm((heads, 2, 4, tt, 2 * HEAD_DIM), BF16),
        vm((heads, 2, tt, 2 * HEAD_DIM), BF16),
        vm((heads, 2, tt, 2 * HEAD_DIM), BF16),
        vm((count, 3 * width), BF16),
        vm((count, half), BF16),
        vm((count, half), BF16),
        vm((2, tt, half), BF16),
        vm((2, tt, half), BF16),
        dma((heads, 8)), dma((heads, 8)),
        dma((heads, 4)), dma((heads, 4)),
        dma((3,)), dma((3,)),
    ]
    if gather:
        n = 2 * nw - 1
        scratch += [dma((2, nw - 1)), dma((2, nw - 1)), dma((n,)), dma((n,)),
                    dma((2 * n,)), dma((2 * n,))]
    mixed, grad_in = pl.pallas_call(
        functools.partial(body, (nh, nw, heads, tt, gather)),
        out_shape=[jax.ShapeDtypeStruct((count, half), BF16)] * 2,
        in_specs=[pl.BlockSpec(memory_space=pltpu.VMEM)] * 6,
        out_specs=[pl.BlockSpec(memory_space=pltpu.VMEM)] * 2,
        scratch_shapes=scratch,
        compiler_params=pltpu.CompilerParams(
            collective_id=0, has_side_effects=True, vmem_limit_bytes=56 * 1024 * 1024),
    )(tokens.reshape(count, model), grad_out.reshape(count, model), weights,
      q_gain.reshape(1, width), k_gain.reshape(1, width), vcol)
    shape = (tile_rows, tile_cols, tt, half)
    return mixed.reshape(shape), grad_in.reshape(shape)


def solution(mesh):
    placed = (
        P("height", "width", None, None),
        P("height", "width", None, None),
        P(("height", "width"), None, "head"),
        P(("height", "width"), "head"),
        P("head"),
        P("head"),
        P("height", "width", None),
    )
    return jax.shard_map(
        functools.partial(on_device, mesh.shape["height"], mesh.shape["width"]),
        mesh=mesh,
        in_specs=placed,
        out_specs=(P("height", "width", None, "head"), P("height", "width", None, "head")),
        check_vma=False,
    )
```

```python
import functools

import jax
import jax.numpy as jnp
from jax import lax
from jax.experimental import pallas as pl
from jax.experimental.pallas import tpu as pltpu
from jax.sharding import PartitionSpec as P

HEAD_DIM = 128
EPS = 1e-06
FACTOR = HEAD_DIM**-0.5
LOG2E = 1.4426950408889634
ABSENT = 1e30
NT = (((1,), (1,)), ((), ()))
TN = (((0,), (0,)), ((), ()))
F32 = jnp.float32
BF16 = jnp.bfloat16


def mm(a, b, dims=(((1,), (0,)), ((), ()))):
    return lax.dot_general(a, b, dims, preferred_element_type=F32)


def body(cfg, *refs):
    nh, nw, heads, tt, gather = cfg
    tok_in, go_in, gains, vcol = refs[:4]
    win = refs[4]
    rest = list(refs[6:] if gather else refs[5:])
    mixed, gin = rest[:2]
    rest = rest[2:]
    W = rest.pop(0) if gather else win
    (raw, ga, qb, kv, kc, gacc, att, gq, gs, gr, gs2, gr2, gqkv, atto, gqkvo, Wo, tok, go) = rest[:18]
    (s_h, r_h, s_g, r_g, s_y, r_y, s_w, r_w, s_in) = rest[18:27]
    tok_copy = pltpu.make_async_copy(tok_in, tok, s_in.at[0])
    go_copy = pltpu.make_async_copy(go_in, go, s_in.at[1])
    tok_copy.start()
    go_copy.start()
    qg, kg = gains.at[0:1], gains.at[1:2]
    width = heads * HEAD_DIM
    h, w, y = lax.axis_index("height"), lax.axis_index("width"), lax.axis_index("head")
    up, down, left, right = h > 0, h < nh - 1, w > 0, w < nw - 1
    peer = (h, w, 1 - y)
    dev = {"u": (h - 1, w, y), "d": (h + 1, w, y), "l": (h, w - 1, y), "r": (h, w + 1, y)}
    there = {"u": up, "d": down, "l": left, "r": right}
    xdev = (lax.rem(h + 2, nh), w, y)
    cdev = (h + 1 - 2 * lax.rem(h, 2), w, y)

    def copy(src, dst, ssem, rsem, to):
        return pltpu.make_async_remote_copy(
            src_ref=src, dst_ref=dst, send_sem=ssem, recv_sem=rsem,
            device_id=to, device_id_type=pl.DeviceIdType.MESH)

    barrier = pltpu.get_barrier_semaphore()

    def greet(to):
        pl.semaphore_signal(barrier, inc=1, device_id=to, device_id_type=pl.DeviceIdType.MESH)

    count = 1
    for side in "udlr":
        pl.when(there[side])(functools.partial(greet, dev[side]))
        count = count + there[side].astype(jnp.int32)
    greet(peer)
    if gather:
        greet(xdev)
        greet(cdev)
        count = count + 2
    pl.semaphore_wait(barrier, count)

    if gather:
        s_z, r_z, s_x, r_x, s_c, r_c, s_v, r_v = rest[27:35]
        rows = win.shape[0]
        total = 2 * nw - 1

        def shard(hh, ww):
            return W.at[pl.ds(pl.multiple_of((hh * nw + ww) * rows, 16), rows), :]

        def column(i):
            if i == 0:
                return w
            k, d = divmod(i - 1, 2)
            return w + 1 + k if d else w - 1 - k

        def held(i):
            if i == 0:
                return w >= 0
            return column(i) < nw if (i - 1) % 2 else column(i) >= 0

        def zc(d, k):
            part = shard(h, w + k if d else w - k)
            return copy(part, part, s_z.at[d, k], r_z.at[d, k], dev["l" if d else "r"])

        def xc(i):
            part = shard(h, column(i))
            return copy(part, part, s_x.at[i], r_x.at[i], xdev)

        def cc(i):
            part = shard(h, column(i)) if i < total else shard(xdev[0], column(i - total))
            return copy(part, part, s_c.at[i], r_c.at[i], cdev)

        core = lax.rem(h, 2)
        mine = h // 2 == 1 - y

        def yc(i):
            to = Wo.at[pl.ds(pl.multiple_of((core * nw + column(i)) * rows, 16), rows), :]
            return copy(shard(2 * (1 - y) + core, column(i)), to, s_w.at[i], r_w.at[i], peer)

        def yv(i):
            part = Wo.at[pl.ds(pl.multiple_of((core * nw + column(i)) * rows, 16), rows), :]
            return copy(part, part, s_v.at[i], r_v.at[i], cdev)

        own_slot = pl.ds(pl.multiple_of((h * nw + w) * rows, 16), rows)
        W[own_slot, 0 : 3 * width] = win[...]
        W[own_slot, 3 * width : 4 * width] = refs[5][...]
        pl.when(right)(lambda: zc(0, 0).start())
        pl.when(left)(lambda: zc(1, 0).start())
        xc(0).start()
        cc(0).start()
        pl.when(mine)(lambda: yc(0).start())
    else:
        half_w = Wo.shape[0]
        w_copy = copy(win.at[pl.ds(pl.multiple_of((1 - y) * half_w, 16), half_w), :], Wo,
                      s_w.at[0], r_w.at[0], peer)
        w_copy.start()

    def fill(index):
        shape = kv.at[index].shape[:-1] + (HEAD_DIM,)
        kv[index + (slice(0, HEAD_DIM),)] = jnp.full(shape, ABSENT, BF16)
        kv[index + (slice(HEAD_DIM, 2 * HEAD_DIM),)] = jnp.zeros(shape, BF16)

    every = slice(None)
    for hd in range(heads):
        for c in range(4):
            pl.when(jnp.logical_not(up))(functools.partial(fill, (hd, c, 0, every)))
            pl.when(jnp.logical_not(down))(functools.partial(fill, (hd, c, 2, every)))
        pl.when(jnp.logical_not(left) & up)(functools.partial(fill, (hd, 0, 0, every)))
        pl.when(jnp.logical_not(right) & up)(functools.partial(fill, (hd, 3, 0, every)))
        pl.when(jnp.logical_not(left) & down)(functools.partial(fill, (hd, 0, 2, every)))
        pl.when(jnp.logical_not(right) & down)(functools.partial(fill, (hd, 3, 2, every)))
        pl.when(jnp.logical_not(left))(functools.partial(fill, (hd, 0, 1, every)))
        pl.when(jnp.logical_not(right))(functools.partial(fill, (hd, 3, 1, every)))

    if gather:
        def pass_x(i):
            xc(i).wait_recv()
            cc(total + i).start()
            pl.when(jnp.logical_not(mine))(lambda: yc(i).start())

        def step(d, k):
            zc(d, k).wait_recv()
            if k + 1 < nw - 1:
                pl.when(left if d else right)(lambda: zc(d, k + 1).start())
            xc(1 + 2 * k + d).start()
            cc(1 + 2 * k + d).start()
            pl.when(mine)(lambda: yc(1 + 2 * k + d).start())

        for k in range(nw - 1):
            for d in range(2):
                pl.when(held(1 + 2 * k + d))(functools.partial(step, d, k))
            for i in ([0] if k == 0 else [2 * k - 1, 2 * k]):
                pl.when(held(i))(functools.partial(pass_x, i))
        for i in (2 * nw - 3, 2 * nw - 2):
            pl.when(held(i))(functools.partial(pass_x, i))
        for i in range(total):
            def done(i=i):
                xc(i).wait_send()
                for j in (i, total + i):
                    cc(j).wait_recv()
                    cc(j).wait_send()
            pl.when(held(i))(done)
        for k in range(nw - 1):
            pl.when(right & (w - k >= 0))(lambda: zc(0, k).wait_send())
            pl.when(left & (w + k < nw))(lambda: zc(1, k).wait_send())

    def tile(hd, c, r):
        return kv.at[hd, c, r]

    def side_copy(hd, side):
        if side == "l":
            return copy(tile(hd, 1, 1), tile(hd, 3, 1), s_h.at[hd, 0], r_h.at[hd, 0], dev["l"])
        if side == "r":
            return copy(tile(hd, 2, 1), tile(hd, 0, 1), s_h.at[hd, 1], r_h.at[hd, 1], dev["r"])
        at, i = (2, 2) if side == "u" else (0, 3)
        return copy(kv.at[hd, pl.ds(1, 2), 1], kv.at[hd, pl.ds(1, 2), at],
                    s_h.at[hd, i], r_h.at[hd, i], dev[side])

    def corner(hd, side, c):
        at, i = (2, 4) if side == "u" else (0, 6)
        i += c // 3
        return copy(tile(hd, c, 1), tile(hd, c, at), s_h.at[hd, i], r_h.at[hd, i], dev[side])

    def sides(hd):
        for side in "lrud":
            pl.when(there[side])(lambda: side_copy(hd, side).start())

    tok_copy.wait()
    raw[:, width:] = mm(tok[...], W[:, width : 3 * width])
    absent = vcol[...] == 0
    for hd in range(heads):
        cols = slice(hd * HEAD_DIM, (hd + 1) * HEAD_DIM)
        k_raw = raw[:, width + hd * HEAD_DIM : width + (hd + 1) * HEAD_DIM]
        inv = lax.rsqrt(jnp.mean(k_raw * k_raw, axis=-1, keepdims=True) + EPS)
        kn = jnp.where(absent, ABSENT, k_raw * inv * kg[:, cols]).astype(BF16)
        v = raw[:, 2 * width + hd * HEAD_DIM : 2 * width + (hd + 1) * HEAD_DIM].astype(BF16)
        for j in range(2):
            kv[hd, 1 + j, 1, :, 0:HEAD_DIM] = kn[j * tt : (j + 1) * tt]
            kv[hd, 1 + j, 1, :, HEAD_DIM:] = v[j * tt : (j + 1) * tt]
        if hd < 2:
            sides(hd)

    go_copy.wait()
    raw[:, 0:width] = mm(tok[...], W[:, 0:width])
    ga[...] = mm(go[...], W[:, 3 * width : 4 * width]).astype(BF16)
    for hd in range(heads):
        cols = slice(hd * HEAD_DIM, (hd + 1) * HEAD_DIM)
        q_raw = raw[:, cols]
        inv = lax.rsqrt(jnp.mean(q_raw * q_raw, axis=-1, keepdims=True) + EPS)
        qb[:, cols] = (q_raw * inv * qg[:, cols]).astype(BF16)

    def forward(hd, side, c):
        side_copy(hd, "r" if c == 0 else "l").wait_recv()
        for s in "ud":
            pl.when(there[s])(lambda: corner(hd, s, c).start())

    def corners(hd):
        pl.when(left)(functools.partial(forward, hd, "l", 0))
        pl.when(right)(functools.partial(forward, hd, "r", 3))

    corners(0)
    for hd in range(2, heads):
        sides(hd)

    def to_peer(part, hd):
        i = part * heads + hd
        if part == 0:
            at = (slice(None), pl.ds(hd * HEAD_DIM, HEAD_DIM))
            return copy(att.at[at], atto.at[at], s_y.at[i], r_y.at[i], peer)
        at = (slice(None), pl.ds((part - 1) * width + hd * HEAD_DIM, HEAD_DIM))
        return copy(gqkv.at[at], gqkvo.at[at], s_y.at[i], r_y.at[i], peer)

    def norm_back(x, gain, g):
        inv = lax.rsqrt(jnp.mean(x * x, axis=-1, keepdims=True) + EPS)
        wg = gain * g
        inner = jnp.mean(wg * x, axis=-1, keepdims=True)
        return (inv * wg - x * (inv * inv * inv) * inner).astype(BF16)

    def back(hd, side):
        i = 0 if side == "u" else 1
        return copy(gs.at[hd, i], gr.at[hd, i], s_g.at[hd, i], r_g.at[hd, i], dev[side])

    def back2(hd, side):
        i = 0 if side == "l" else 1
        return copy(gs2.at[hd, i], gr2.at[hd, i], s_g.at[hd, 2 + i], r_g.at[hd, 2 + i], dev[side])

    win_rows = 9 * tt
    for hd in range(heads):
        cols = slice(hd * HEAD_DIM, (hd + 1) * HEAD_DIM)
        if hd + 1 < heads:
            corners(hd + 1)
        for side, other in (("d", "u"), ("u", "d")):
            def arrived(side=side, other=other):
                side_copy(hd, other).wait_recv()
                pl.when(left)(lambda: corner(hd, other, 0).wait_recv())
                pl.when(right)(lambda: corner(hd, other, 3).wait_recv())
            pl.when(there[side])(arrived)
        keys = kv[hd, :, :, :, 0:HEAD_DIM].reshape(12 * tt, HEAD_DIM).astype(F32)
        out = keys > ABSENT * 0.1
        kc[:, 0:HEAD_DIM] = jnp.where(out, 0.0, keys).astype(BF16)
        kc[:, HEAD_DIM:] = jnp.where(out, -1e9, 0.0).astype(BF16)
        for j in range(2):
            rows_j = slice(j * tt, (j + 1) * tt)
            span = slice(3 * j * tt, 3 * j * tt + win_rows)
            q = qb[rows_j, cols]
            up_ = ga[rows_j, cols]
            both = kc[span, :]
            values = kv[hd, j : j + 3, :, :, HEAD_DIM:].reshape(win_rows, HEAD_DIM)
            s = mm(jnp.concatenate([q, jnp.ones_like(q)], axis=1), both, NT)
            e = jnp.exp2(s * (FACTOR * LOG2E))
            p = e * (1.0 / jnp.sum(e, axis=-1, keepdims=True))
            pb = p.astype(BF16)
            att[rows_j, cols] = mm(pb, values).astype(BF16)
            gp = mm(up_, values, NT)
            ds = (p * (gp - jnp.sum(p * gp, axis=-1, keepdims=True))).astype(BF16)
            gq[rows_j, cols] = mm(ds, both[:, 0:HEAD_DIM]) * FACTOR
            dk = mm(ds, q, TN) * FACTOR
            dv = mm(pb, up_, TN)
            if j == 0:
                gacc[hd, 0:win_rows, 0:HEAD_DIM] = dk
                gacc[hd, 0:win_rows, HEAD_DIM:] = dv
            else:
                lo = 3 * tt
                gacc[hd, lo:win_rows, 0:HEAD_DIM] += dk[: win_rows - lo]
                gacc[hd, lo:win_rows, HEAD_DIM:] += dv[: win_rows - lo]
                gacc[hd, win_rows:, 0:HEAD_DIM] = dk[win_rows - lo :]
                gacc[hd, win_rows:, HEAD_DIM:] = dv[win_rows - lo :]
        for i, side in ((0, "u"), (1, "d")):
            for c in range(4):
                at = (3 * c + 2 * i) * tt
                gs[hd, i, c] = gacc[hd, at : at + tt, :].astype(BF16)
            pl.when(there[side])(lambda: back(hd, side).start())
        to_peer(0, hd).start()
        gqkv[:, cols] = norm_back(raw[:, cols], qg[:, cols], gq[:, cols])
        to_peer(1, hd).start()

    half = gin.shape[1]
    own_rows = pl.ds(pl.multiple_of(y * half, 128), half)
    if gather:
        def pass_w(i):
            yc(i).wait_recv()
            yv(i).start()

        for i in range(total):
            pl.when(held(i))(functools.partial(pass_w, i))

    for hd in range(heads):
        for i, (side, other) in enumerate((("u", "d"), ("d", "u"))):
            def add(i=i, side=side, other=other):
                back(hd, other).wait_recv()
                for c in range(4):
                    at = (3 * c + 1) * tt
                    gacc[hd, at : at + tt, :] += gr[hd, 1 - i, c].astype(F32)
            pl.when(there[side])(add)
        for i, (side, c) in enumerate((("l", 0), ("r", 3))):
            def send(i=i, side=side, c=c):
                at = (3 * c + 1) * tt
                gs2[hd, i] = gacc[hd, at : at + tt, :].astype(BF16)
                back2(hd, side).start()
            pl.when(there[side])(send)

    out_cols = slice(3 * width, 4 * width)
    own_mixed = mm(att[...], W[own_rows, out_cols], NT)
    if gather:
        def weights_in(i):
            yv(i).wait_recv()
            yv(i).wait_send()
            yc(i).wait_send()

        for i in range(total):
            pl.when(held(i))(functools.partial(weights_in, i))
    else:
        w_copy.wait_recv()
    for hd in range(heads):
        to_peer(0, hd).wait_recv()
    mixed[...] = (own_mixed + mm(atto[...], Wo[:, out_cols], NT)).astype(BF16)

    for hd in range(heads):
        for i, (side, other, c) in enumerate((("l", "r", 1), ("r", "l", 2))):
            def add2(i=i, other=other, c=c):
                back2(hd, other).wait_recv()
                at = (3 * c + 1) * tt
                gacc[hd, at : at + tt, :] += gr2[hd, 1 - i].astype(F32)
            pl.when(there[side])(add2)
        cols = slice(hd * HEAD_DIM, (hd + 1) * HEAD_DIM)
        kcols = slice(width + hd * HEAD_DIM, width + (hd + 1) * HEAD_DIM)
        vcols = slice(2 * width + hd * HEAD_DIM, 2 * width + (hd + 1) * HEAD_DIM)
        for j in range(2):
            rows_j = slice(j * tt, (j + 1) * tt)
            at = (3 * (1 + j) + 1) * tt
            gqkv[rows_j, kcols] = norm_back(
                raw[rows_j, kcols], kg[:, cols], gacc[hd, at : at + tt, 0:HEAD_DIM])
            gqkv[rows_j, vcols] = gacc[hd, at : at + tt, HEAD_DIM:].astype(BF16)
        to_peer(2, hd).start()
        to_peer(3, hd).start()

    for hd in range(heads):
        to_peer(1, hd).wait_recv()
        if hd + 1 < heads:
            to_peer(2, hd).wait_recv()
            to_peer(3, hd).wait_recv()
    early = (slice(0, 2 * width - HEAD_DIM), slice(2 * width, 3 * width - HEAD_DIM))
    late = (slice(2 * width - HEAD_DIM, 2 * width), slice(3 * width - HEAD_DIM, 3 * width))
    total_in = mm(gqkv[...], W[own_rows, 0 : 3 * width], NT)
    for part in early:
        total_in += mm(gqkvo[:, part], Wo[:, part], NT)
    to_peer(2, heads - 1).wait_recv()
    to_peer(3, heads - 1).wait_recv()
    for part in late:
        total_in += mm(gqkvo[:, part], Wo[:, part], NT)
    gin[...] = total_in.astype(BF16)

    if not gather:
        w_copy.wait_send()
    for hd in range(heads):
        for part in range(4):
            to_peer(part, hd).wait_send()
        for side in "lrud":
            pl.when(there[side])(lambda: side_copy(hd, side).wait_send())
        for s in "ud":
            pl.when(there[s] & left)(lambda: corner(hd, s, 0).wait_send())
            pl.when(there[s] & right)(lambda: corner(hd, s, 3).wait_send())
            pl.when(there[s])(lambda: back(hd, s).wait_send())
        for s in "lr":
            pl.when(there[s])(lambda: back2(hd, s).wait_send())


def on_device(nh, nw, tokens, grad_out, qkv_weight, out_weight, q_gain, k_gain, key_valid):
    tile_rows, tile_cols, tt, model = tokens.shape
    count = tile_rows * tile_cols * tt
    width = q_gain.shape[0]
    heads = width // HEAD_DIM
    weights = [qkv_weight.reshape(qkv_weight.shape[0], 3 * width), out_weight]
    gather = nh == 4 and nw > 1 and out_weight.shape[0] % 16 == 0
    if not gather:
        whole = jnp.concatenate(weights, axis=1)
        weights = [lax.all_gather(whole, ("height", "width"), axis=0, tiled=True)]
    vcol = jnp.broadcast_to(key_valid.astype(F32).reshape(count, 1), (count, HEAD_DIM))
    half = model // 2
    vm = pltpu.VMEM
    dma = pltpu.SemaphoreType.DMA
    scratch = [vm((model, 4 * width), BF16)] if gather else []
    scratch += [
        vm((count, 3 * width), F32),
        vm((count, width), BF16),
        vm((count, width), BF16),
        vm((heads, 4, 3, tt, 2 * HEAD_DIM), BF16),
        vm((12 * tt, 2 * HEAD_DIM), BF16),
        vm((heads, 12 * tt, 2 * HEAD_DIM), F32),
        vm((count, width), BF16),
        vm((count, width), F32),
        vm((heads, 2, 4, tt, 2 * HEAD_DIM), BF16),
        vm((heads, 2, 4, tt, 2 * HEAD_DIM), BF16),
        vm((heads, 2, tt, 2 * HEAD_DIM), BF16),
        vm((heads, 2, tt, 2 * HEAD_DIM), BF16),
        vm((count, 3 * width), BF16),
        vm((count, width), BF16),
        vm((count, 3 * width), BF16),
        vm((half, 4 * width), BF16),
        vm((count, model), BF16),
        vm((count, model), BF16),
        dma((heads, 8)), dma((heads, 8)),
        dma((heads, 4)), dma((heads, 4)),
        dma((4 * heads,)), dma((4 * heads,)),
        dma((2 * nw - 1,)), dma((2 * nw - 1,)),
        dma((2,)),
    ]
    if gather:
        n = 2 * nw - 1
        scratch += [dma((2, nw - 1)), dma((2, nw - 1)), dma((n,)), dma((n,)),
                    dma((2 * n,)), dma((2 * n,)), dma((n,)), dma((n,))]
    mixed, grad_in = pl.pallas_call(
        functools.partial(body, (nh, nw, heads, tt, gather)),
        out_shape=[jax.ShapeDtypeStruct((count, half), BF16)] * 2,
        in_specs=[pl.BlockSpec(memory_space=pl.ANY)] * 2
        + [pl.BlockSpec(memory_space=pltpu.VMEM)] * (2 + len(weights)),
        out_specs=[pl.BlockSpec(memory_space=pltpu.VMEM)] * 2,
        scratch_shapes=scratch,
        compiler_params=pltpu.CompilerParams(
            collective_id=0, has_side_effects=True, vmem_limit_bytes=56 * 1024 * 1024),
    )(tokens.reshape(count, model), grad_out.reshape(count, model),
      jnp.stack([q_gain, k_gain]), vcol, *weights)
    shape = (tile_rows, tile_cols, tt, half)
    return mixed.reshape(shape), grad_in.reshape(shape)


def solution(mesh):
    placed = (
        P("height", "width", None, None),
        P("height", "width", None, None),
        P(("height", "width"), None, "head"),
        P(("height", "width"), "head"),
        P("head"),
        P("head"),
        P("height", "width", None),
    )
    return jax.shard_map(
        functools.partial(on_device, mesh.shape["height"], mesh.shape["width"]),
        mesh=mesh,
        in_specs=placed,
        out_specs=(P("height", "width", None, "head"), P("height", "width", None, "head")),
        check_vma=False,
    )
```

```python
import functools

import jax
import jax.numpy as jnp
from jax import lax
from jax.experimental import pallas as pl
from jax.experimental.pallas import tpu as pltpu
from jax.sharding import PartitionSpec as P

HEAD_DIM = 128
EPS = 1e-06
FACTOR = HEAD_DIM**-0.5
LOG2E = 1.4426950408889634
ABSENT = 1e30
NT = (((1,), (1,)), ((), ()))
TN = (((0,), (0,)), ((), ()))
F32 = jnp.float32
BF16 = jnp.bfloat16


def mm(a, b, dims=(((1,), (0,)), ((), ()))):
    return lax.dot_general(a, b, dims, preferred_element_type=F32)


def body(cfg, *refs):
    nh, nw, heads, tt, gather = cfg
    tok_in, go_in, gains, vcol = refs[:4]
    win = refs[4]
    rest = list(refs[6:] if gather else refs[5:])
    mixed, gin = rest[:2]
    rest = rest[2:]
    W = rest.pop(0) if gather else win
    (raw, ga, qb, kv, kc, gacc, att, gq, gs, gr, gs2, gr2, gqkv, atto, gqkvo, Wo, tok, go) = rest[:18]
    (s_h, r_h, s_g, r_g, s_y, r_y, s_w, r_w, s_in) = rest[18:27]
    tok_copy = pltpu.make_async_copy(tok_in, tok, s_in.at[0])
    go_copy = pltpu.make_async_copy(go_in, go, s_in.at[1])
    tok_copy.start()
    go_copy.start()
    qg, kg = gains.at[0:1], gains.at[1:2]
    width = heads * HEAD_DIM
    h, w, y = lax.axis_index("height"), lax.axis_index("width"), lax.axis_index("head")
    up, down, left, right = h > 0, h < nh - 1, w > 0, w < nw - 1
    peer = (h, w, 1 - y)
    dev = {"u": (h - 1, w, y), "d": (h + 1, w, y), "l": (h, w - 1, y), "r": (h, w + 1, y)}
    there = {"u": up, "d": down, "l": left, "r": right}
    xdev = (lax.rem(h + 2, nh), w, y)
    cdev = (h + 1 - 2 * lax.rem(h, 2), w, y)

    def copy(src, dst, ssem, rsem, to):
        return pltpu.make_async_remote_copy(
            src_ref=src, dst_ref=dst, send_sem=ssem, recv_sem=rsem,
            device_id=to, device_id_type=pl.DeviceIdType.MESH)

    barrier = pltpu.get_barrier_semaphore()

    def greet(to):
        pl.semaphore_signal(barrier, inc=1, device_id=to, device_id_type=pl.DeviceIdType.MESH)

    count = 1
    for side in "udlr":
        pl.when(there[side])(functools.partial(greet, dev[side]))
        count = count + there[side].astype(jnp.int32)
    greet(peer)
    if gather:
        greet(xdev)
        greet(cdev)
        count = count + 2
    pl.semaphore_wait(barrier, count)

    if gather:
        s_z, r_z, s_x, r_x, s_c, r_c, s_v, r_v = rest[27:35]
        rows = win.shape[0]
        total = 2 * nw - 1

        def shard(hh, ww, part=None):
            at = pl.ds(pl.multiple_of((hh * nw + ww) * rows, 16), rows)
            if part is None:
                return W.at[at, :]
            return W.at[at, pl.ds(2 * width * part, 2 * width)]

        def column(i):
            if i == 0:
                return w
            k, d = divmod(i - 1, 2)
            return w + 1 + k if d else w - 1 - k

        def held(i):
            if i == 0:
                return w >= 0
            return column(i) < nw if (i - 1) % 2 else column(i) >= 0

        def zc(p, d, k):
            part = shard(h, w + k if d else w - k, p)
            return copy(part, part, s_z.at[p, d, k], r_z.at[p, d, k], dev["l" if d else "r"])

        def xc(p, i):
            part = shard(h, column(i), p)
            return copy(part, part, s_x.at[p, i], r_x.at[p, i], xdev)

        def cc(p, i):
            hh, i_ = (h, i) if i < total else (xdev[0], i - total)
            part = shard(hh, column(i_), p)
            return copy(part, part, s_c.at[p, i], r_c.at[p, i], cdev)

        core = lax.rem(h, 2)
        mine = h // 2 == 1 - y

        def yc(i):
            to = Wo.at[pl.ds(pl.multiple_of((core * nw + column(i)) * rows, 16), rows), :]
            return copy(shard(2 * (1 - y) + core, column(i)), to, s_w.at[i], r_w.at[i], peer)

        def yv(i):
            part = Wo.at[pl.ds(pl.multiple_of((core * nw + column(i)) * rows, 16), rows), :]
            return copy(part, part, s_v.at[i], r_v.at[i], cdev)

        own_slot = pl.ds(pl.multiple_of((h * nw + w) * rows, 16), rows)
        W[own_slot, 0 : 2 * width] = win[:, width : 3 * width]
        W[own_slot, 2 * width : 3 * width] = win[:, 0:width]
        W[own_slot, 3 * width : 4 * width] = refs[5][...]

        def begin(p):
            pl.when(right)(lambda: zc(p, 0, 0).start())
            pl.when(left)(lambda: zc(p, 1, 0).start())
            xc(p, 0).start()
            cc(p, 0).start()
            if p:
                pl.when(mine)(lambda: yc(0).start())

        def pass_x(p, i):
            xc(p, i).wait_recv()
            cc(p, total + i).start()
            if p:
                pl.when(jnp.logical_not(mine))(lambda: yc(i).start())

        def step(p, d, k):
            zc(p, d, k).wait_recv()
            if k + 1 < nw - 1:
                pl.when(left if d else right)(lambda: zc(p, d, k + 1).start())
            i = 1 + 2 * k + d
            xc(p, i).start()
            cc(p, i).start()
            if p:
                pl.when(mine)(lambda: yc(i).start())

        def stage(p, k):
            for d in range(2):
                pl.when(held(1 + 2 * k + d))(functools.partial(step, p, d, k))
            for i in ([0] if k == 0 else [2 * k - 1, 2 * k]):
                pl.when(held(i))(functools.partial(pass_x, p, i))

        def finish(p):
            for i in (2 * nw - 3, 2 * nw - 2):
                pl.when(held(i))(functools.partial(pass_x, p, i))

            def done(i):
                cc(p, i).wait_recv()
                cc(p, total + i).wait_recv()

            for i in range(total):
                pl.when(held(i))(functools.partial(done, i))

        def sent(p):
            def done(i):
                xc(p, i).wait_send()
                cc(p, i).wait_send()
                cc(p, total + i).wait_send()

            for i in range(total):
                pl.when(held(i))(functools.partial(done, i))
            for k in range(nw - 1):
                pl.when(right & (w - k >= 0))(lambda: zc(p, 0, k).wait_send())
                pl.when(left & (w + k < nw))(lambda: zc(p, 1, k).wait_send())

        begin(0)
    else:
        half_w = Wo.shape[0]
        w_copy = copy(win.at[pl.ds(pl.multiple_of((1 - y) * half_w, 16), half_w), :], Wo,
                      s_w.at[0], r_w.at[0], peer)
        w_copy.start()

    def fill(index):
        shape = kv.at[index].shape[:-1] + (HEAD_DIM,)
        kv[index + (slice(0, HEAD_DIM),)] = jnp.full(shape, ABSENT, BF16)
        kv[index + (slice(HEAD_DIM, 2 * HEAD_DIM),)] = jnp.zeros(shape, BF16)

    every = slice(None)
    for hd in range(heads):
        for c in range(4):
            pl.when(jnp.logical_not(up))(functools.partial(fill, (hd, c, 0, every)))
            pl.when(jnp.logical_not(down))(functools.partial(fill, (hd, c, 2, every)))
        pl.when(jnp.logical_not(left) & up)(functools.partial(fill, (hd, 0, 0, every)))
        pl.when(jnp.logical_not(right) & up)(functools.partial(fill, (hd, 3, 0, every)))
        pl.when(jnp.logical_not(left) & down)(functools.partial(fill, (hd, 0, 2, every)))
        pl.when(jnp.logical_not(right) & down)(functools.partial(fill, (hd, 3, 2, every)))
        pl.when(jnp.logical_not(left))(functools.partial(fill, (hd, 0, 1, every)))
        pl.when(jnp.logical_not(right))(functools.partial(fill, (hd, 3, 1, every)))

    if gather:
        for k in range(nw - 1):
            stage(0, k)
        begin(1)
        finish(0)

    def tile(hd, c, r):
        return kv.at[hd, c, r]

    def side_copy(hd, side):
        if side == "l":
            return copy(tile(hd, 1, 1), tile(hd, 3, 1), s_h.at[hd, 0], r_h.at[hd, 0], dev["l"])
        if side == "r":
            return copy(tile(hd, 2, 1), tile(hd, 0, 1), s_h.at[hd, 1], r_h.at[hd, 1], dev["r"])
        at, i = (2, 2) if side == "u" else (0, 3)
        return copy(kv.at[hd, pl.ds(1, 2), 1], kv.at[hd, pl.ds(1, 2), at],
                    s_h.at[hd, i], r_h.at[hd, i], dev[side])

    def corner(hd, side, c):
        at, i = (2, 4) if side == "u" else (0, 6)
        i += c // 3
        return copy(tile(hd, c, 1), tile(hd, c, at), s_h.at[hd, i], r_h.at[hd, i], dev[side])

    def sides(hd):
        for side in "lrud":
            pl.when(there[side])(lambda: side_copy(hd, side).start())

    tok_copy.wait()
    raw[:, 0 : 2 * width] = mm(tok[...], W[:, 0 : 2 * width])
    absent = vcol[...] == 0
    for hd in range(heads):
        cols = slice(hd * HEAD_DIM, (hd + 1) * HEAD_DIM)
        k_raw = raw[:, cols]
        inv = lax.rsqrt(jnp.mean(k_raw * k_raw, axis=-1, keepdims=True) + EPS)
        kn = jnp.where(absent, ABSENT, k_raw * inv * kg[:, cols]).astype(BF16)
        v = raw[:, width + hd * HEAD_DIM : width + (hd + 1) * HEAD_DIM].astype(BF16)
        for j in range(2):
            kv[hd, 1 + j, 1, :, 0:HEAD_DIM] = kn[j * tt : (j + 1) * tt]
            kv[hd, 1 + j, 1, :, HEAD_DIM:] = v[j * tt : (j + 1) * tt]
        if hd < 2:
            sides(hd)

    def forward(hd, side, c):
        side_copy(hd, "r" if c == 0 else "l").wait_recv()
        for s in "ud":
            pl.when(there[s])(lambda: corner(hd, s, c).start())

    def corners(hd):
        pl.when(left)(functools.partial(forward, hd, "l", 0))
        pl.when(right)(functools.partial(forward, hd, "r", 3))

    for k in range(max(nw - 1, heads)):
        if gather and k < nw - 1:
            stage(1, k)
        if k + 2 < heads:
            sides(k + 2)
        if k < heads - 1:
            corners(k)
    if gather:
        finish(1)

    go_copy.wait()
    raw[:, 2 * width :] = mm(tok[...], W[:, 2 * width : 3 * width])
    ga[...] = mm(go[...], W[:, 3 * width : 4 * width]).astype(BF16)
    for hd in range(heads):
        cols = slice(hd * HEAD_DIM, (hd + 1) * HEAD_DIM)
        q_raw = raw[:, 2 * width + hd * HEAD_DIM : 2 * width + (hd + 1) * HEAD_DIM]
        inv = lax.rsqrt(jnp.mean(q_raw * q_raw, axis=-1, keepdims=True) + EPS)
        qb[:, cols] = (q_raw * inv * qg[:, cols]).astype(BF16)

    def to_peer(part, hd):
        i = part * heads + hd
        if part == 0:
            at = (slice(None), pl.ds(hd * HEAD_DIM, HEAD_DIM))
            return copy(att.at[at], atto.at[at], s_y.at[i], r_y.at[i], peer)
        base = (2 * width, 0, width)[part - 1]
        at = (slice(None), pl.ds(base + hd * HEAD_DIM, HEAD_DIM))
        return copy(gqkv.at[at], gqkvo.at[at], s_y.at[i], r_y.at[i], peer)

    def norm_back(x, gain, g):
        inv = lax.rsqrt(jnp.mean(x * x, axis=-1, keepdims=True) + EPS)
        wg = gain * g
        inner = jnp.mean(wg * x, axis=-1, keepdims=True)
        return (inv * wg - x * (inv * inv * inv) * inner).astype(BF16)

    def back(hd, side):
        i = 0 if side == "u" else 1
        return copy(gs.at[hd, i], gr.at[hd, i], s_g.at[hd, i], r_g.at[hd, i], dev[side])

    def back2(hd, side):
        i = 0 if side == "l" else 1
        return copy(gs2.at[hd, i], gr2.at[hd, i], s_g.at[hd, 2 + i], r_g.at[hd, 2 + i], dev[side])

    win_rows = 9 * tt
    for hd in range(heads):
        cols = slice(hd * HEAD_DIM, (hd + 1) * HEAD_DIM)
        if hd == 0:
            corners(heads - 1)
        for side, other in (("d", "u"), ("u", "d")):
            def arrived(side=side, other=other):
                side_copy(hd, other).wait_recv()
                pl.when(left)(lambda: corner(hd, other, 0).wait_recv())
                pl.when(right)(lambda: corner(hd, other, 3).wait_recv())
            pl.when(there[side])(arrived)
        keys = kv[hd, :, :, :, 0:HEAD_DIM].reshape(12 * tt, HEAD_DIM).astype(F32)
        out = keys > ABSENT * 0.1
        kc[:, 0:HEAD_DIM] = jnp.where(out, 0.0, keys).astype(BF16)
        kc[:, HEAD_DIM:] = jnp.where(out, -1e9, 0.0).astype(BF16)
        for j in range(2):
            rows_j = slice(j * tt, (j + 1) * tt)
            span = slice(3 * j * tt, 3 * j * tt + win_rows)
            q = qb[rows_j, cols]
            up_ = ga[rows_j, cols]
            both = kc[span, :]
            values = kv[hd, j : j + 3, :, :, HEAD_DIM:].reshape(win_rows, HEAD_DIM)
            s = mm(jnp.concatenate([q, jnp.ones_like(q)], axis=1), both, NT)
            e = jnp.exp2(s * (FACTOR * LOG2E))
            p = e * (1.0 / jnp.sum(e, axis=-1, keepdims=True))
            pb = p.astype(BF16)
            att[rows_j, cols] = mm(pb, values).astype(BF16)
            gp = mm(up_, values, NT)
            ds = (p * (gp - jnp.sum(p * gp, axis=-1, keepdims=True))).astype(BF16)
            gq[rows_j, cols] = mm(ds, both[:, 0:HEAD_DIM]) * FACTOR
            dk = mm(ds, q, TN) * FACTOR
            dv = mm(pb, up_, TN)
            if j == 0:
                gacc[hd, 0:win_rows, 0:HEAD_DIM] = dk
                gacc[hd, 0:win_rows, HEAD_DIM:] = dv
            else:
                lo = 3 * tt
                gacc[hd, lo:win_rows, 0:HEAD_DIM] += dk[: win_rows - lo]
                gacc[hd, lo:win_rows, HEAD_DIM:] += dv[: win_rows - lo]
                gacc[hd, win_rows:, 0:HEAD_DIM] = dk[win_rows - lo :]
                gacc[hd, win_rows:, HEAD_DIM:] = dv[win_rows - lo :]
        for i, side in ((0, "u"), (1, "d")):
            for c in range(4):
                at = (3 * c + 2 * i) * tt
                gs[hd, i, c] = gacc[hd, at : at + tt, :].astype(BF16)
            pl.when(there[side])(lambda: back(hd, side).start())
        to_peer(0, hd).start()
        qcols = slice(2 * width + hd * HEAD_DIM, 2 * width + (hd + 1) * HEAD_DIM)
        gqkv[:, qcols] = norm_back(raw[:, qcols], qg[:, cols], gq[:, cols])
        to_peer(1, hd).start()

    half = gin.shape[1]
    own_rows = pl.ds(pl.multiple_of(y * half, 128), half)
    if gather:
        def pass_w(i):
            yc(i).wait_recv()
            yv(i).start()

        for i in range(total):
            pl.when(held(i))(functools.partial(pass_w, i))

    for hd in range(heads):
        for i, (side, other) in enumerate((("u", "d"), ("d", "u"))):
            def add(i=i, side=side, other=other):
                back(hd, other).wait_recv()
                for c in range(4):
                    at = (3 * c + 1) * tt
                    gacc[hd, at : at + tt, :] += gr[hd, 1 - i, c].astype(F32)
            pl.when(there[side])(add)
        for i, (side, c) in enumerate((("l", 0), ("r", 3))):
            def send(i=i, side=side, c=c):
                at = (3 * c + 1) * tt
                gs2[hd, i] = gacc[hd, at : at + tt, :].astype(BF16)
                back2(hd, side).start()
            pl.when(there[side])(send)

    out_cols = slice(3 * width, 4 * width)
    own_mixed = mm(att[...], W[own_rows, out_cols], NT)
    if gather:
        def weights_in(i):
            yv(i).wait_recv()
            yv(i).wait_send()
            yc(i).wait_send()

        for i in range(total):
            pl.when(held(i))(functools.partial(weights_in, i))
    else:
        w_copy.wait_recv()
    for hd in range(heads):
        to_peer(0, hd).wait_recv()
    mixed[...] = (own_mixed + mm(atto[...], Wo[:, out_cols], NT)).astype(BF16)

    for hd in range(heads):
        for i, (side, other, c) in enumerate((("l", "r", 1), ("r", "l", 2))):
            def add2(i=i, other=other, c=c):
                back2(hd, other).wait_recv()
                at = (3 * c + 1) * tt
                gacc[hd, at : at + tt, :] += gr2[hd, 1 - i].astype(F32)
            pl.when(there[side])(add2)
        cols = slice(hd * HEAD_DIM, (hd + 1) * HEAD_DIM)
        kcols = cols
        vcols = slice(width + hd * HEAD_DIM, width + (hd + 1) * HEAD_DIM)
        for j in range(2):
            rows_j = slice(j * tt, (j + 1) * tt)
            at = (3 * (1 + j) + 1) * tt
            gqkv[rows_j, kcols] = norm_back(
                raw[rows_j, kcols], kg[:, cols], gacc[hd, at : at + tt, 0:HEAD_DIM])
            gqkv[rows_j, vcols] = gacc[hd, at : at + tt, HEAD_DIM:].astype(BF16)
        to_peer(2, hd).start()
        to_peer(3, hd).start()

    for hd in range(heads):
        to_peer(1, hd).wait_recv()
        if hd + 1 < heads:
            to_peer(2, hd).wait_recv()
            to_peer(3, hd).wait_recv()
    early = (slice(0, width - HEAD_DIM), slice(width, 2 * width - HEAD_DIM),
             slice(2 * width, 3 * width))
    late = (slice(width - HEAD_DIM, width), slice(2 * width - HEAD_DIM, 2 * width))
    total_in = mm(gqkv[...], W[own_rows, 0 : 3 * width], NT)
    for part in early:
        total_in += mm(gqkvo[:, part], Wo[:, part], NT)
    to_peer(2, heads - 1).wait_recv()
    to_peer(3, heads - 1).wait_recv()
    for part in late:
        total_in += mm(gqkvo[:, part], Wo[:, part], NT)
    gin[...] = total_in.astype(BF16)

    if gather:
        sent(0)
        sent(1)
    else:
        w_copy.wait_send()
    for hd in range(heads):
        for part in range(4):
            to_peer(part, hd).wait_send()
        for side in "lrud":
            pl.when(there[side])(lambda: side_copy(hd, side).wait_send())
        for s in "ud":
            pl.when(there[s] & left)(lambda: corner(hd, s, 0).wait_send())
            pl.when(there[s] & right)(lambda: corner(hd, s, 3).wait_send())
            pl.when(there[s])(lambda: back(hd, s).wait_send())
        for s in "lr":
            pl.when(there[s])(lambda: back2(hd, s).wait_send())


def on_device(nh, nw, tokens, grad_out, qkv_weight, out_weight, q_gain, k_gain, key_valid):
    tile_rows, tile_cols, tt, model = tokens.shape
    count = tile_rows * tile_cols * tt
    width = q_gain.shape[0]
    heads = width // HEAD_DIM
    weights = [qkv_weight.reshape(qkv_weight.shape[0], 3 * width), out_weight]
    gather = nh == 4 and nw > 1 and out_weight.shape[0] % 16 == 0
    if not gather:
        ordered = [weights[0][:, width:], weights[0][:, :width], out_weight]
        whole = jnp.concatenate(ordered, axis=1)
        weights = [lax.all_gather(whole, ("height", "width"), axis=0, tiled=True)]
    vcol = jnp.broadcast_to(key_valid.astype(F32).reshape(count, 1), (count, HEAD_DIM))
    half = model // 2
    vm = pltpu.VMEM
    dma = pltpu.SemaphoreType.DMA
    scratch = [vm((model, 4 * width), BF16)] if gather else []
    scratch += [
        vm((count, 3 * width), F32),
        vm((count, width), BF16),
        vm((count, width), BF16),
        vm((heads, 4, 3, tt, 2 * HEAD_DIM), BF16),
        vm((12 * tt, 2 * HEAD_DIM), BF16),
        vm((heads, 12 * tt, 2 * HEAD_DIM), F32),
        vm((count, width), BF16),
        vm((count, width), F32),
        vm((heads, 2, 4, tt, 2 * HEAD_DIM), BF16),
        vm((heads, 2, 4, tt, 2 * HEAD_DIM), BF16),
        vm((heads, 2, tt, 2 * HEAD_DIM), BF16),
        vm((heads, 2, tt, 2 * HEAD_DIM), BF16),
        vm((count, 3 * width), BF16),
        vm((count, width), BF16),
        vm((count, 3 * width), BF16),
        vm((half, 4 * width), BF16),
        vm((count, model), BF16),
        vm((count, model), BF16),
        dma((heads, 8)), dma((heads, 8)),
        dma((heads, 4)), dma((heads, 4)),
        dma((4 * heads,)), dma((4 * heads,)),
        dma((2 * nw - 1,)), dma((2 * nw - 1,)),
        dma((2,)),
    ]
    if gather:
        n = 2 * nw - 1
        scratch += [dma((2, 2, nw - 1)), dma((2, 2, nw - 1)), dma((2, n)), dma((2, n)),
                    dma((2, 2 * n)), dma((2, 2 * n)), dma((n,)), dma((n,))]
    mixed, grad_in = pl.pallas_call(
        functools.partial(body, (nh, nw, heads, tt, gather)),
        out_shape=[jax.ShapeDtypeStruct((count, half), BF16)] * 2,
        in_specs=[pl.BlockSpec(memory_space=pl.ANY)] * 2
        + [pl.BlockSpec(memory_space=pltpu.VMEM)] * (2 + len(weights)),
        out_specs=[pl.BlockSpec(memory_space=pltpu.VMEM)] * 2,
        scratch_shapes=scratch,
        compiler_params=pltpu.CompilerParams(
            collective_id=0, has_side_effects=True, vmem_limit_bytes=56 * 1024 * 1024),
    )(tokens.reshape(count, model), grad_out.reshape(count, model),
      jnp.stack([q_gain, k_gain]), vcol, *weights)
    shape = (tile_rows, tile_cols, tt, half)
    return mixed.reshape(shape), grad_in.reshape(shape)


def solution(mesh):
    placed = (
        P("height", "width", None, None),
        P("height", "width", None, None),
        P(("height", "width"), None, "head"),
        P(("height", "width"), "head"),
        P("head"),
        P("head"),
        P("height", "width", None),
    )
    return jax.shard_map(
        functools.partial(on_device, mesh.shape["height"], mesh.shape["width"]),
        mesh=mesh,
        in_specs=placed,
        out_specs=(P("height", "width", None, "head"), P("height", "width", None, "head")),
        check_vma=False,
    )
```

```python
import functools

import jax
import jax.numpy as jnp
from jax import lax
from jax.experimental import pallas as pl
from jax.experimental.pallas import tpu as pltpu
from jax.sharding import PartitionSpec as P

HEAD_DIM = 128
EPS = 1e-06
FACTOR = HEAD_DIM**-0.5
LOG2E = 1.4426950408889634
ABSENT = 1e30
NT = (((1,), (1,)), ((), ()))
TN = (((0,), (0,)), ((), ()))
F32 = jnp.float32
BF16 = jnp.bfloat16


def mm(a, b, dims=(((1,), (0,)), ((), ()))):
    return lax.dot_general(a, b, dims, preferred_element_type=F32)


def body(cfg, *refs):
    nh, nw, heads, tt, gather = cfg
    tok_in, go_in, q_gain, k_gain, vcol = refs[:5]
    win = refs[5]
    rest = list(refs[7:] if gather else refs[6:])
    mixed, gin = rest[:2]
    rest = rest[2:]
    W = rest.pop(0) if gather else win
    (raw, ga, qb, kv, kc, gacc, att, gq, gs, gr, gs2, gr2, gqkv, atto, gqkvo, Wo, tok, go) = rest[:18]
    (s_h, r_h, s_g, r_g, s_y, r_y, s_w, r_w, s_in) = rest[18:27]
    tok_copy = pltpu.make_async_copy(tok_in, tok, s_in.at[0])
    go_copy = pltpu.make_async_copy(go_in, go, s_in.at[1])
    tok_copy.start()
    go_copy.start()
    qg, kg = q_gain[...].reshape(1, -1), k_gain[...].reshape(1, -1)
    width = heads * HEAD_DIM
    h, w, y = lax.axis_index("height"), lax.axis_index("width"), lax.axis_index("head")
    up, down, left, right = h > 0, h < nh - 1, w > 0, w < nw - 1
    peer = (h, w, 1 - y)
    dev = {"u": (h - 1, w, y), "d": (h + 1, w, y), "l": (h, w - 1, y), "r": (h, w + 1, y)}
    there = {"u": up, "d": down, "l": left, "r": right}
    xdev = (lax.rem(h + 2, nh), w, y)
    cdev = (h + 1 - 2 * lax.rem(h, 2), w, y)

    def copy(src, dst, ssem, rsem, to):
        return pltpu.make_async_remote_copy(
            src_ref=src, dst_ref=dst, send_sem=ssem, recv_sem=rsem,
            device_id=to, device_id_type=pl.DeviceIdType.MESH)

    barrier = pltpu.get_barrier_semaphore()

    def greet(to):
        pl.semaphore_signal(barrier, inc=1, device_id=to, device_id_type=pl.DeviceIdType.MESH)

    count = 1
    for side in "udlr":
        pl.when(there[side])(functools.partial(greet, dev[side]))
        count = count + there[side].astype(jnp.int32)
    greet(peer)
    if gather:
        greet(xdev)
        greet(cdev)
        count = count + 2
    pl.semaphore_wait(barrier, count)

    if gather:
        s_z, r_z, s_x, r_x, s_c, r_c, s_v, r_v = rest[27:35]
        rows = win.shape[0]
        total = 2 * nw - 1

        def shard(hh, ww):
            return W.at[pl.ds(pl.multiple_of((hh * nw + ww) * rows, 16), rows), :]

        def column(i):
            if i == 0:
                return w
            k, d = divmod(i - 1, 2)
            return w + 1 + k if d else w - 1 - k

        def held(i):
            if i == 0:
                return w >= 0
            return column(i) < nw if (i - 1) % 2 else column(i) >= 0

        def zc(d, k):
            part = shard(h, w + k if d else w - k)
            return copy(part, part, s_z.at[d, k], r_z.at[d, k], dev["l" if d else "r"])

        def xc(i):
            part = shard(h, column(i))
            return copy(part, part, s_x.at[i], r_x.at[i], xdev)

        def cc(i):
            part = shard(h, column(i)) if i < total else shard(xdev[0], column(i - total))
            return copy(part, part, s_c.at[i], r_c.at[i], cdev)

        core = lax.rem(h, 2)
        mine = h // 2 == 1 - y

        def yc(i):
            to = Wo.at[pl.ds(pl.multiple_of((core * nw + column(i)) * rows, 16), rows), :]
            return copy(shard(2 * (1 - y) + core, column(i)), to, s_w.at[i], r_w.at[i], peer)

        def yv(i):
            part = Wo.at[pl.ds(pl.multiple_of((core * nw + column(i)) * rows, 16), rows), :]
            return copy(part, part, s_v.at[i], r_v.at[i], cdev)

        own_slot = pl.ds(pl.multiple_of((h * nw + w) * rows, 16), rows)
        W[own_slot, 0 : 3 * width] = win[...]
        W[own_slot, 3 * width : 4 * width] = refs[6][...]
        pl.when(right)(lambda: zc(0, 0).start())
        pl.when(left)(lambda: zc(1, 0).start())
        xc(0).start()
        cc(0).start()
        pl.when(mine)(lambda: yc(0).start())
    else:
        half_w = Wo.shape[0]
        w_copy = copy(win.at[pl.ds(pl.multiple_of((1 - y) * half_w, 16), half_w), :], Wo,
                      s_w.at[0], r_w.at[0], peer)
        w_copy.start()

    def fill(index):
        shape = kv.at[index].shape[:-1] + (HEAD_DIM,)
        kv[index + (slice(0, HEAD_DIM),)] = jnp.full(shape, ABSENT, BF16)
        kv[index + (slice(HEAD_DIM, 2 * HEAD_DIM),)] = jnp.zeros(shape, BF16)

    every = slice(None)
    for hd in range(heads):
        for c in range(4):
            pl.when(jnp.logical_not(up))(functools.partial(fill, (hd, c, 0, every)))
            pl.when(jnp.logical_not(down))(functools.partial(fill, (hd, c, 2, every)))
        pl.when(jnp.logical_not(left) & up)(functools.partial(fill, (hd, 0, 0, every)))
        pl.when(jnp.logical_not(right) & up)(functools.partial(fill, (hd, 3, 0, every)))
        pl.when(jnp.logical_not(left) & down)(functools.partial(fill, (hd, 0, 2, every)))
        pl.when(jnp.logical_not(right) & down)(functools.partial(fill, (hd, 3, 2, every)))
        pl.when(jnp.logical_not(left))(functools.partial(fill, (hd, 0, 1, every)))
        pl.when(jnp.logical_not(right))(functools.partial(fill, (hd, 3, 1, every)))

    if gather:
        def pass_x(i):
            xc(i).wait_recv()
            cc(total + i).start()
            pl.when(jnp.logical_not(mine))(lambda: yc(i).start())

        def step(d, k):
            zc(d, k).wait_recv()
            if k + 1 < nw - 1:
                pl.when(left if d else right)(lambda: zc(d, k + 1).start())
            xc(1 + 2 * k + d).start()
            cc(1 + 2 * k + d).start()
            pl.when(mine)(lambda: yc(1 + 2 * k + d).start())

        for k in range(nw - 1):
            for d in range(2):
                pl.when(held(1 + 2 * k + d))(functools.partial(step, d, k))
            for i in ([0] if k == 0 else [2 * k - 1, 2 * k]):
                pl.when(held(i))(functools.partial(pass_x, i))
        def block(hh):
            at = pl.ds(pl.multiple_of(hh * nw * rows, 128), nw * rows)
            return mm(tok[:, at], W[at, width : 3 * width])

        tok_copy.wait()
        raw[:, width:] = block(h)
        for i in range(total):
            pl.when(held(i))(lambda: cc(i).wait_recv())
        raw[:, width:] += block(cdev[0])
        for i in (2 * nw - 3, 2 * nw - 2):
            pl.when(held(i))(functools.partial(pass_x, i))
        raw[:, width:] += block(xdev[0])
        for i in range(total):
            pl.when(held(i))(lambda: cc(total + i).wait_recv())
        raw[:, width:] += block(lax.rem(cdev[0] + 2, nh))

        def all_sent():
            def done(i):
                xc(i).wait_send()
                cc(i).wait_send()
                cc(total + i).wait_send()

            for i in range(total):
                pl.when(held(i))(functools.partial(done, i))
            for k in range(nw - 1):
                pl.when(right & (w - k >= 0))(lambda: zc(0, k).wait_send())
                pl.when(left & (w + k < nw))(lambda: zc(1, k).wait_send())

    def tile(hd, c, r):
        return kv.at[hd, c, r]

    def side_copy(hd, side):
        if side == "l":
            return copy(tile(hd, 1, 1), tile(hd, 3, 1), s_h.at[hd, 0], r_h.at[hd, 0], dev["l"])
        if side == "r":
            return copy(tile(hd, 2, 1), tile(hd, 0, 1), s_h.at[hd, 1], r_h.at[hd, 1], dev["r"])
        at, i = (2, 2) if side == "u" else (0, 3)
        return copy(kv.at[hd, pl.ds(1, 2), 1], kv.at[hd, pl.ds(1, 2), at],
                    s_h.at[hd, i], r_h.at[hd, i], dev[side])

    def corner(hd, side, c):
        at, i = (2, 4) if side == "u" else (0, 6)
        i += c // 3
        return copy(tile(hd, c, 1), tile(hd, c, at), s_h.at[hd, i], r_h.at[hd, i], dev[side])

    def sides(hd):
        for side in "lrud":
            pl.when(there[side])(lambda: side_copy(hd, side).start())

    if not gather:
        tok_copy.wait()
        raw[:, width:] = mm(tok[...], W[:, width : 3 * width])
    absent = vcol[...] == 0
    for hd in range(heads):
        cols = slice(hd * HEAD_DIM, (hd + 1) * HEAD_DIM)
        k_raw = raw[:, width + hd * HEAD_DIM : width + (hd + 1) * HEAD_DIM]
        inv = lax.rsqrt(jnp.mean(k_raw * k_raw, axis=-1, keepdims=True) + EPS)
        kn = jnp.where(absent, ABSENT, k_raw * inv * kg[:, cols]).astype(BF16)
        v = raw[:, 2 * width + hd * HEAD_DIM : 2 * width + (hd + 1) * HEAD_DIM].astype(BF16)
        for j in range(2):
            kv[hd, 1 + j, 1, :, 0:HEAD_DIM] = kn[j * tt : (j + 1) * tt]
            kv[hd, 1 + j, 1, :, HEAD_DIM:] = v[j * tt : (j + 1) * tt]
        if hd < 2:
            sides(hd)

    go_copy.wait()
    raw[:, 0:width] = mm(tok[...], W[:, 0:width])
    ga[...] = mm(go[...], W[:, 3 * width : 4 * width]).astype(BF16)
    for hd in range(heads):
        cols = slice(hd * HEAD_DIM, (hd + 1) * HEAD_DIM)
        q_raw = raw[:, cols]
        inv = lax.rsqrt(jnp.mean(q_raw * q_raw, axis=-1, keepdims=True) + EPS)
        qb[:, cols] = (q_raw * inv * qg[:, cols]).astype(BF16)

    def forward(hd, side, c):
        side_copy(hd, "r" if c == 0 else "l").wait_recv()
        for s in "ud":
            pl.when(there[s])(lambda: corner(hd, s, c).start())

    def corners(hd):
        pl.when(left)(functools.partial(forward, hd, "l", 0))
        pl.when(right)(functools.partial(forward, hd, "r", 3))

    corners(0)
    for hd in range(2, heads):
        sides(hd)

    def to_peer(part, hd):
        i = part * heads + hd
        if part == 0:
            at = (slice(None), pl.ds(hd * HEAD_DIM, HEAD_DIM))
            return copy(att.at[at], atto.at[at], s_y.at[i], r_y.at[i], peer)
        at = (slice(None), pl.ds((part - 1) * width + hd * HEAD_DIM, HEAD_DIM))
        return copy(gqkv.at[at], gqkvo.at[at], s_y.at[i], r_y.at[i], peer)

    def norm_back(x, gain, g):
        inv = lax.rsqrt(jnp.mean(x * x, axis=-1, keepdims=True) + EPS)
        wg = gain * g
        inner = jnp.mean(wg * x, axis=-1, keepdims=True)
        return (inv * wg - x * (inv * inv * inv) * inner).astype(BF16)

    def back(hd, side):
        i = 0 if side == "u" else 1
        return copy(gs.at[hd, i], gr.at[hd, i], s_g.at[hd, i], r_g.at[hd, i], dev[side])

    def back2(hd, side):
        i = 0 if side == "l" else 1
        return copy(gs2.at[hd, i], gr2.at[hd, i], s_g.at[hd, 2 + i], r_g.at[hd, 2 + i], dev[side])

    win_rows = 9 * tt
    for hd in range(heads):
        cols = slice(hd * HEAD_DIM, (hd + 1) * HEAD_DIM)
        if hd + 1 < heads:
            corners(hd + 1)
        for side, other in (("d", "u"), ("u", "d")):
            def arrived(side=side, other=other):
                side_copy(hd, other).wait_recv()
                pl.when(left)(lambda: corner(hd, other, 0).wait_recv())
                pl.when(right)(lambda: corner(hd, other, 3).wait_recv())
            pl.when(there[side])(arrived)
        keys = kv[hd, :, :, :, 0:HEAD_DIM].reshape(12 * tt, HEAD_DIM).astype(F32)
        out = keys > ABSENT * 0.1
        kc[:, 0:HEAD_DIM] = jnp.where(out, 0.0, keys).astype(BF16)
        kc[:, HEAD_DIM:] = jnp.where(out, -1e9, 0.0).astype(BF16)
        for j in range(2):
            rows_j = slice(j * tt, (j + 1) * tt)
            span = slice(3 * j * tt, 3 * j * tt + win_rows)
            q = qb[rows_j, cols]
            up_ = ga[rows_j, cols]
            both = kc[span, :]
            values = kv[hd, j : j + 3, :, :, HEAD_DIM:].reshape(win_rows, HEAD_DIM)
            s = mm(jnp.concatenate([q, jnp.ones_like(q)], axis=1), both, NT)
            e = jnp.exp2(s * (FACTOR * LOG2E))
            p = e * (1.0 / jnp.sum(e, axis=-1, keepdims=True))
            pb = p.astype(BF16)
            att[rows_j, cols] = mm(pb, values).astype(BF16)
            gp = mm(up_, values, NT)
            ds = (p * (gp - jnp.sum(p * gp, axis=-1, keepdims=True))).astype(BF16)
            gq[rows_j, cols] = mm(ds, both[:, 0:HEAD_DIM]) * FACTOR
            dk = mm(ds, q, TN) * FACTOR
            dv = mm(pb, up_, TN)
            if j == 0:
                gacc[hd, 0:win_rows, 0:HEAD_DIM] = dk
                gacc[hd, 0:win_rows, HEAD_DIM:] = dv
            else:
                lo = 3 * tt
                gacc[hd, lo:win_rows, 0:HEAD_DIM] += dk[: win_rows - lo]
                gacc[hd, lo:win_rows, HEAD_DIM:] += dv[: win_rows - lo]
                gacc[hd, win_rows:, 0:HEAD_DIM] = dk[win_rows - lo :]
                gacc[hd, win_rows:, HEAD_DIM:] = dv[win_rows - lo :]
        for i, side in ((0, "u"), (1, "d")):
            for c in range(4):
                at = (3 * c + 2 * i) * tt
                gs[hd, i, c] = gacc[hd, at : at + tt, :].astype(BF16)
            pl.when(there[side])(lambda: back(hd, side).start())
        to_peer(0, hd).start()
        gqkv[:, cols] = norm_back(raw[:, cols], qg[:, cols], gq[:, cols])
        to_peer(1, hd).start()

    half = gin.shape[1]
    own_rows = pl.ds(pl.multiple_of(y * half, 128), half)
    if gather:
        def pass_w(i):
            yc(i).wait_recv()
            yv(i).start()

        for i in range(total):
            pl.when(held(i))(functools.partial(pass_w, i))

    for hd in range(heads):
        for i, (side, other) in enumerate((("u", "d"), ("d", "u"))):
            def add(i=i, side=side, other=other):
                back(hd, other).wait_recv()
                for c in range(4):
                    at = (3 * c + 1) * tt
                    gacc[hd, at : at + tt, :] += gr[hd, 1 - i, c].astype(F32)
            pl.when(there[side])(add)
        for i, (side, c) in enumerate((("l", 0), ("r", 3))):
            def send(i=i, side=side, c=c):
                at = (3 * c + 1) * tt
                gs2[hd, i] = gacc[hd, at : at + tt, :].astype(BF16)
                back2(hd, side).start()
            pl.when(there[side])(send)

    out_cols = slice(3 * width, 4 * width)
    own_mixed = mm(att[...], W[own_rows, out_cols], NT)
    if gather:
        def weights_in(i):
            yv(i).wait_recv()
            yv(i).wait_send()
            yc(i).wait_send()

        for i in range(total):
            pl.when(held(i))(functools.partial(weights_in, i))
    else:
        w_copy.wait_recv()
    for hd in range(heads):
        to_peer(0, hd).wait_recv()
    mixed[...] = (own_mixed + mm(atto[...], Wo[:, out_cols], NT)).astype(BF16)

    for hd in range(heads):
        for i, (side, other, c) in enumerate((("l", "r", 1), ("r", "l", 2))):
            def add2(i=i, other=other, c=c):
                back2(hd, other).wait_recv()
                at = (3 * c + 1) * tt
                gacc[hd, at : at + tt, :] += gr2[hd, 1 - i].astype(F32)
            pl.when(there[side])(add2)
        cols = slice(hd * HEAD_DIM, (hd + 1) * HEAD_DIM)
        kcols = slice(width + hd * HEAD_DIM, width + (hd + 1) * HEAD_DIM)
        vcols = slice(2 * width + hd * HEAD_DIM, 2 * width + (hd + 1) * HEAD_DIM)
        for j in range(2):
            rows_j = slice(j * tt, (j + 1) * tt)
            at = (3 * (1 + j) + 1) * tt
            gqkv[rows_j, kcols] = norm_back(
                raw[rows_j, kcols], kg[:, cols], gacc[hd, at : at + tt, 0:HEAD_DIM])
            gqkv[rows_j, vcols] = gacc[hd, at : at + tt, HEAD_DIM:].astype(BF16)
        to_peer(2, hd).start()
        to_peer(3, hd).start()

    for hd in range(heads):
        to_peer(1, hd).wait_recv()
        if hd + 1 < heads:
            to_peer(2, hd).wait_recv()
            to_peer(3, hd).wait_recv()
    early = (slice(0, 2 * width - HEAD_DIM), slice(2 * width, 3 * width - HEAD_DIM))
    late = (slice(2 * width - HEAD_DIM, 2 * width), slice(3 * width - HEAD_DIM, 3 * width))
    total_in = mm(gqkv[...], W[own_rows, 0 : 3 * width], NT)
    for part in early:
        total_in += mm(gqkvo[:, part], Wo[:, part], NT)
    to_peer(2, heads - 1).wait_recv()
    to_peer(3, heads - 1).wait_recv()
    for part in late:
        total_in += mm(gqkvo[:, part], Wo[:, part], NT)
    gin[...] = total_in.astype(BF16)

    if gather:
        all_sent()
    else:
        w_copy.wait_send()
    for hd in range(heads):
        for part in range(4):
            to_peer(part, hd).wait_send()
        for side in "lrud":
            pl.when(there[side])(lambda: side_copy(hd, side).wait_send())
        for s in "ud":
            pl.when(there[s] & left)(lambda: corner(hd, s, 0).wait_send())
            pl.when(there[s] & right)(lambda: corner(hd, s, 3).wait_send())
            pl.when(there[s])(lambda: back(hd, s).wait_send())
        for s in "lr":
            pl.when(there[s])(lambda: back2(hd, s).wait_send())


def on_device(nh, nw, tokens, grad_out, qkv_weight, out_weight, q_gain, k_gain, key_valid):
    tile_rows, tile_cols, tt, model = tokens.shape
    count = tile_rows * tile_cols * tt
    width = q_gain.shape[0]
    heads = width // HEAD_DIM
    weights = [qkv_weight.reshape(qkv_weight.shape[0], 3 * width), out_weight]
    gather = nh == 4 and nw > 1 and out_weight.shape[0] % 32 == 0
    if not gather:
        whole = jnp.concatenate(weights, axis=1)
        weights = [lax.all_gather(whole, ("height", "width"), axis=0, tiled=True)]
    vcol = jnp.broadcast_to(key_valid.astype(F32).reshape(count, 1), (count, HEAD_DIM))
    half = model // 2
    vm = pltpu.VMEM
    dma = pltpu.SemaphoreType.DMA
    scratch = [vm((model, 4 * width), BF16)] if gather else []
    scratch += [
        vm((count, 3 * width), F32),
        vm((count, width), BF16),
        vm((count, width), BF16),
        vm((heads, 4, 3, tt, 2 * HEAD_DIM), BF16),
        vm((12 * tt, 2 * HEAD_DIM), BF16),
        vm((heads, 12 * tt, 2 * HEAD_DIM), F32),
        vm((count, width), BF16),
        vm((count, width), F32),
        vm((heads, 2, 4, tt, 2 * HEAD_DIM), BF16),
        vm((heads, 2, 4, tt, 2 * HEAD_DIM), BF16),
        vm((heads, 2, tt, 2 * HEAD_DIM), BF16),
        vm((heads, 2, tt, 2 * HEAD_DIM), BF16),
        vm((count, 3 * width), BF16),
        vm((count, width), BF16),
        vm((count, 3 * width), BF16),
        vm((half, 4 * width), BF16),
        vm((count, model), BF16),
        vm((count, model), BF16),
        dma((heads, 8)), dma((heads, 8)),
        dma((heads, 4)), dma((heads, 4)),
        dma((4 * heads,)), dma((4 * heads,)),
        dma((2 * nw - 1,)), dma((2 * nw - 1,)),
        dma((2,)),
    ]
    if gather:
        n = 2 * nw - 1
        scratch += [dma((2, nw - 1)), dma((2, nw - 1)), dma((n,)), dma((n,)),
                    dma((2 * n,)), dma((2 * n,)), dma((n,)), dma((n,))]
    mixed, grad_in = pl.pallas_call(
        functools.partial(body, (nh, nw, heads, tt, gather)),
        out_shape=[jax.ShapeDtypeStruct((count, half), BF16)] * 2,
        in_specs=[pl.BlockSpec(memory_space=pl.ANY)] * 2
        + [pl.BlockSpec(memory_space=pltpu.VMEM)] * (3 + len(weights)),
        out_specs=[pl.BlockSpec(memory_space=pltpu.VMEM)] * 2,
        scratch_shapes=scratch,
        compiler_params=pltpu.CompilerParams(
            collective_id=0, has_side_effects=True, vmem_limit_bytes=56 * 1024 * 1024),
    )(tokens.reshape(count, model), grad_out.reshape(count, model),
      q_gain, k_gain, vcol, *weights)
    shape = (tile_rows, tile_cols, tt, half)
    return mixed.reshape(shape), grad_in.reshape(shape)


def solution(mesh):
    placed = (
        P("height", "width", None, None),
        P("height", "width", None, None),
        P(("height", "width"), None, "head"),
        P(("height", "width"), "head"),
        P("head"),
        P("head"),
        P("height", "width", None),
    )
    return jax.shard_map(
        functools.partial(on_device, mesh.shape["height"], mesh.shape["width"]),
        mesh=mesh,
        in_specs=placed,
        out_specs=(P("height", "width", None, "head"), P("height", "width", None, "head")),
        check_vma=False,
    )
```

```python
import functools

import jax
import jax.numpy as jnp
from jax import lax
from jax.experimental import pallas as pl
from jax.experimental.pallas import tpu as pltpu
from jax.sharding import PartitionSpec as P

HEAD_DIM = 128
EPS = 1e-06
FACTOR = HEAD_DIM**-0.5
LOG2E = 1.4426950408889634
ABSENT = 1e30
NT = (((1,), (1,)), ((), ()))
TN = (((0,), (0,)), ((), ()))
F32 = jnp.float32
BF16 = jnp.bfloat16


def mm(a, b, dims=(((1,), (0,)), ((), ()))):
    return lax.dot_general(a, b, dims, preferred_element_type=F32)


def body(cfg, *refs):
    nh, nw, heads, tt, gather = cfg
    tok_in, go_in, q_gain, k_gain, vcol = refs[:5]
    win = refs[5]
    rest = list(refs[7:] if gather else refs[6:])
    mixed, gin = rest[:2]
    rest = rest[2:]
    W = rest.pop(0) if gather else win
    (raw, ga, qb, kv, kc, gacc, att, gq, gs, gr, gs2, gr2, gqkv, atto, gqkvo, Wo, tok, go) = rest[:18]
    (s_h, r_h, s_g, r_g, s_y, r_y, s_w, r_w, s_in) = rest[18:27]
    tok_copy = pltpu.make_async_copy(tok_in, tok, s_in.at[0])
    go_copy = pltpu.make_async_copy(go_in, go, s_in.at[1])
    tok_copy.start()
    go_copy.start()
    qg, kg = q_gain[...].reshape(1, -1), k_gain[...].reshape(1, -1)
    width = heads * HEAD_DIM
    h, w, y = lax.axis_index("height"), lax.axis_index("width"), lax.axis_index("head")
    up, down, left, right = h > 0, h < nh - 1, w > 0, w < nw - 1
    peer = (h, w, 1 - y)
    dev = {"u": (h - 1, w, y), "d": (h + 1, w, y), "l": (h, w - 1, y), "r": (h, w + 1, y)}
    there = {"u": up, "d": down, "l": left, "r": right}
    xdev = (lax.rem(h + 2, nh), w, y)
    cdev = (h + 1 - 2 * lax.rem(h, 2), w, y)

    def copy(src, dst, ssem, rsem, to):
        return pltpu.make_async_remote_copy(
            src_ref=src, dst_ref=dst, send_sem=ssem, recv_sem=rsem,
            device_id=to, device_id_type=pl.DeviceIdType.MESH)

    barrier = pltpu.get_barrier_semaphore()

    def greet(to):
        pl.semaphore_signal(barrier, inc=1, device_id=to, device_id_type=pl.DeviceIdType.MESH)

    count = 1
    for side in "udlr":
        pl.when(there[side])(functools.partial(greet, dev[side]))
        count = count + there[side].astype(jnp.int32)
    greet(peer)
    if gather:
        greet(xdev)
        greet(cdev)
        count = count + 2
    pl.semaphore_wait(barrier, count)

    if gather:
        s_z, r_z, s_x, r_x, s_c, r_c, s_v, r_v = rest[27:35]
        rows = win.shape[0]
        total = 2 * nw - 1

        def shard(hh, ww):
            return W.at[pl.ds(pl.multiple_of((hh * nw + ww) * rows, 16), rows), :]

        def column(i):
            if i == 0:
                return w
            k, d = divmod(i - 1, 2)
            return w + 1 + k if d else w - 1 - k

        def held(i):
            if i == 0:
                return w >= 0
            return column(i) < nw if (i - 1) % 2 else column(i) >= 0

        def zc(d, k):
            part = shard(h, w + k if d else w - k)
            return copy(part, part, s_z.at[d, k], r_z.at[d, k], dev["l" if d else "r"])

        def xc(i):
            part = shard(h, column(i))
            return copy(part, part, s_x.at[i], r_x.at[i], xdev)

        def cc(i):
            part = shard(h, column(i)) if i < total else shard(xdev[0], column(i - total))
            return copy(part, part, s_c.at[i], r_c.at[i], cdev)

        core = lax.rem(h, 2)
        mine = h // 2 == 1 - y

        def yc(i):
            to = Wo.at[pl.ds(pl.multiple_of((core * nw + column(i)) * rows, 16), rows), :]
            return copy(shard(2 * (1 - y) + core, column(i)), to, s_w.at[i], r_w.at[i], peer)

        def yv(i):
            part = Wo.at[pl.ds(pl.multiple_of((core * nw + column(i)) * rows, 16), rows), :]
            return copy(part, part, s_v.at[i], r_v.at[i], cdev)

        own_slot = pl.ds(pl.multiple_of((h * nw + w) * rows, 16), rows)
        W[own_slot, 0 : 3 * width] = win[...]
        W[own_slot, 3 * width : 4 * width] = refs[6][...]
        pl.when(right)(lambda: zc(0, 0).start())
        pl.when(left)(lambda: zc(1, 0).start())
        xc(0).start()
        cc(0).start()
        pl.when(mine)(lambda: yc(0).start())
    else:
        half_w = Wo.shape[0]
        w_copy = copy(win.at[pl.ds(pl.multiple_of((1 - y) * half_w, 16), half_w), :], Wo,
                      s_w.at[0], r_w.at[0], peer)
        w_copy.start()

    def fill(index):
        shape = kv.at[index].shape[:-1] + (HEAD_DIM,)
        kv[index + (slice(0, HEAD_DIM),)] = jnp.full(shape, ABSENT, BF16)
        kv[index + (slice(HEAD_DIM, 2 * HEAD_DIM),)] = jnp.zeros(shape, BF16)

    every = slice(None)
    for hd in range(heads):
        for c in range(4):
            pl.when(jnp.logical_not(up))(functools.partial(fill, (hd, c, 0, every)))
            pl.when(jnp.logical_not(down))(functools.partial(fill, (hd, c, 2, every)))
        pl.when(jnp.logical_not(left) & up)(functools.partial(fill, (hd, 0, 0, every)))
        pl.when(jnp.logical_not(right) & up)(functools.partial(fill, (hd, 3, 0, every)))
        pl.when(jnp.logical_not(left) & down)(functools.partial(fill, (hd, 0, 2, every)))
        pl.when(jnp.logical_not(right) & down)(functools.partial(fill, (hd, 3, 2, every)))
        pl.when(jnp.logical_not(left))(functools.partial(fill, (hd, 0, 1, every)))
        pl.when(jnp.logical_not(right))(functools.partial(fill, (hd, 3, 1, every)))

    if gather:
        def pass_x(i):
            xc(i).wait_recv()
            cc(total + i).start()
            pl.when(jnp.logical_not(mine))(lambda: yc(i).start())

        def step(d, k):
            zc(d, k).wait_recv()
            if k + 1 < nw - 1:
                pl.when(left if d else right)(lambda: zc(d, k + 1).start())
            xc(1 + 2 * k + d).start()
            cc(1 + 2 * k + d).start()
            pl.when(mine)(lambda: yc(1 + 2 * k + d).start())

        for k in range(nw - 1):
            for d in range(2):
                pl.when(held(1 + 2 * k + d))(functools.partial(step, d, k))
            for i in ([0] if k == 0 else [2 * k - 1, 2 * k]):
                pl.when(held(i))(functools.partial(pass_x, i))
        def block(hh):
            at = pl.ds(pl.multiple_of(hh * nw * rows, 128), nw * rows)
            return mm(tok[:, at], W[at, width : 3 * width])

        tok_copy.wait()
        raw[:, width:] = block(h)
        for i in range(total):
            pl.when(held(i))(lambda: cc(i).wait_recv())
        raw[:, width:] += block(cdev[0])
        for i in (2 * nw - 3, 2 * nw - 2):
            pl.when(held(i))(functools.partial(pass_x, i))
        raw[:, width:] += block(xdev[0])
        for i in range(total):
            pl.when(held(i))(lambda: cc(total + i).wait_recv())
        raw[:, width:] += block(lax.rem(cdev[0] + 2, nh))

        def all_sent():
            def done(i):
                xc(i).wait_send()
                cc(i).wait_send()
                cc(total + i).wait_send()

            for i in range(total):
                pl.when(held(i))(functools.partial(done, i))
            for k in range(nw - 1):
                pl.when(right & (w - k >= 0))(lambda: zc(0, k).wait_send())
                pl.when(left & (w + k < nw))(lambda: zc(1, k).wait_send())

    def tile(hd, c, r):
        return kv.at[hd, c, r]

    def side_copy(hd, side):
        if side == "l":
            return copy(tile(hd, 1, 1), tile(hd, 3, 1), s_h.at[hd, 0], r_h.at[hd, 0], dev["l"])
        if side == "r":
            return copy(tile(hd, 2, 1), tile(hd, 0, 1), s_h.at[hd, 1], r_h.at[hd, 1], dev["r"])
        at, i = (2, 2) if side == "u" else (0, 3)
        return copy(kv.at[hd, pl.ds(1, 2), 1], kv.at[hd, pl.ds(1, 2), at],
                    s_h.at[hd, i], r_h.at[hd, i], dev[side])

    def corner(hd, side, c):
        at, i = (2, 4) if side == "u" else (0, 6)
        i += c // 3
        return copy(tile(hd, c, 1), tile(hd, c, at), s_h.at[hd, i], r_h.at[hd, i], dev[side])

    def sides(hd):
        for side in "lrud":
            pl.when(there[side])(lambda: side_copy(hd, side).start())

    if not gather:
        tok_copy.wait()
        raw[:, width:] = mm(tok[...], W[:, width : 3 * width])
    absent = vcol[...] == 0
    for hd in range(heads):
        cols = slice(hd * HEAD_DIM, (hd + 1) * HEAD_DIM)
        k_raw = raw[:, width + hd * HEAD_DIM : width + (hd + 1) * HEAD_DIM]
        inv = lax.rsqrt(jnp.mean(k_raw * k_raw, axis=-1, keepdims=True) + EPS)
        kn = jnp.where(absent, ABSENT, k_raw * inv * kg[:, cols]).astype(BF16)
        v = raw[:, 2 * width + hd * HEAD_DIM : 2 * width + (hd + 1) * HEAD_DIM].astype(BF16)
        for j in range(2):
            kv[hd, 1 + j, 1, :, 0:HEAD_DIM] = kn[j * tt : (j + 1) * tt]
            kv[hd, 1 + j, 1, :, HEAD_DIM:] = v[j * tt : (j + 1) * tt]
        if hd < 2:
            sides(hd)

    go_copy.wait()
    raw[:, 0:width] = mm(tok[...], W[:, 0:width])
    ga[...] = mm(go[...], W[:, 3 * width : 4 * width]).astype(BF16)
    for hd in range(heads):
        cols = slice(hd * HEAD_DIM, (hd + 1) * HEAD_DIM)
        q_raw = raw[:, cols]
        inv = lax.rsqrt(jnp.mean(q_raw * q_raw, axis=-1, keepdims=True) + EPS)
        qb[:, cols] = (q_raw * inv * qg[:, cols]).astype(BF16)

    def forward(hd, side, c):
        side_copy(hd, "r" if c == 0 else "l").wait_recv()
        for s in "ud":
            pl.when(there[s])(lambda: corner(hd, s, c).start())

    def corners(hd):
        pl.when(left)(functools.partial(forward, hd, "l", 0))
        pl.when(right)(functools.partial(forward, hd, "r", 3))

    corners(0)
    for hd in range(2, heads):
        sides(hd)

    def to_peer(part, hd):
        i = part * heads + hd
        if part == 0:
            at = (slice(None), pl.ds(hd * HEAD_DIM, HEAD_DIM))
            return copy(att.at[at], atto.at[at], s_y.at[i], r_y.at[i], peer)
        at = (slice(None), pl.ds((part - 1) * width + hd * HEAD_DIM, HEAD_DIM))
        return copy(gqkv.at[at], gqkvo.at[at], s_y.at[i], r_y.at[i], peer)

    def norm_back(x, gain, g):
        inv = lax.rsqrt(jnp.mean(x * x, axis=-1, keepdims=True) + EPS)
        wg = gain * g
        inner = jnp.mean(wg * x, axis=-1, keepdims=True)
        return (inv * wg - x * (inv * inv * inv) * inner).astype(BF16)

    def back(hd, side):
        i = 0 if side == "u" else 1
        return copy(gs.at[hd, i], gr.at[hd, i], s_g.at[hd, i], r_g.at[hd, i], dev[side])

    def back2(hd, side):
        i = 0 if side == "l" else 1
        return copy(gs2.at[hd, i], gr2.at[hd, i], s_g.at[hd, 2 + i], r_g.at[hd, 2 + i], dev[side])

    win_rows = 9 * tt
    for hd in range(heads):
        cols = slice(hd * HEAD_DIM, (hd + 1) * HEAD_DIM)
        if hd + 1 < heads:
            corners(hd + 1)
        for side, other in (("d", "u"), ("u", "d")):
            def arrived(side=side, other=other):
                side_copy(hd, other).wait_recv()
                pl.when(left)(lambda: corner(hd, other, 0).wait_recv())
                pl.when(right)(lambda: corner(hd, other, 3).wait_recv())
            pl.when(there[side])(arrived)
        keys = kv[hd, :, :, :, 0:HEAD_DIM].reshape(12 * tt, HEAD_DIM).astype(F32)
        out = keys > ABSENT * 0.1
        kc[:, 0:HEAD_DIM] = jnp.where(out, 0.0, keys).astype(BF16)
        kc[:, HEAD_DIM:] = jnp.where(out, -1e9, 0.0).astype(BF16)
        for j in range(2):
            rows_j = slice(j * tt, (j + 1) * tt)
            span = slice(3 * j * tt, 3 * j * tt + win_rows)
            q = qb[rows_j, cols]
            up_ = ga[rows_j, cols]
            both = kc[span, :]
            values = kv[hd, j : j + 3, :, :, HEAD_DIM:].reshape(win_rows, HEAD_DIM)
            s = mm(jnp.concatenate([q, jnp.ones_like(q)], axis=1), both, NT)
            e = jnp.exp2(s * (FACTOR * LOG2E))
            p = e * (1.0 / jnp.sum(e, axis=-1, keepdims=True))
            pb = p.astype(BF16)
            att[rows_j, cols] = mm(pb, values).astype(BF16)
            gp = mm(up_, values, NT)
            ds = (p * (gp - jnp.sum(p * gp, axis=-1, keepdims=True))).astype(BF16)
            gq[rows_j, cols] = mm(ds, both[:, 0:HEAD_DIM]) * FACTOR
            dk = mm(ds, q, TN) * FACTOR
            dv = mm(pb, up_, TN)
            if j == 0:
                gacc[hd, 0:win_rows, 0:HEAD_DIM] = dk
                gacc[hd, 0:win_rows, HEAD_DIM:] = dv
            else:
                lo = 3 * tt
                gacc[hd, lo:win_rows, 0:HEAD_DIM] += dk[: win_rows - lo]
                gacc[hd, lo:win_rows, HEAD_DIM:] += dv[: win_rows - lo]
                gacc[hd, win_rows:, 0:HEAD_DIM] = dk[win_rows - lo :]
                gacc[hd, win_rows:, HEAD_DIM:] = dv[win_rows - lo :]
        for i, side in ((0, "u"), (1, "d")):
            for c in range(4):
                at = (3 * c + 2 * i) * tt
                gs[hd, i, c] = gacc[hd, at : at + tt, :].astype(BF16)
            pl.when(there[side])(lambda: back(hd, side).start())
        to_peer(0, hd).start()
        gqkv[:, cols] = norm_back(raw[:, cols], qg[:, cols], gq[:, cols])
        to_peer(1, hd).start()

    half = gin.shape[1]
    own_rows = pl.ds(pl.multiple_of(y * half, 128), half)
    if gather:
        def pass_w(i):
            yc(i).wait_recv()
            yv(i).start()

        for i in range(total):
            pl.when(held(i))(functools.partial(pass_w, i))

    for hd in range(heads):
        for i, (side, other) in enumerate((("u", "d"), ("d", "u"))):
            def add(i=i, side=side, other=other):
                back(hd, other).wait_recv()
                for c in range(4):
                    at = (3 * c + 1) * tt
                    gacc[hd, at : at + tt, :] += gr[hd, 1 - i, c].astype(F32)
            pl.when(there[side])(add)
        for i, (side, c) in enumerate((("l", 0), ("r", 3))):
            def send(i=i, side=side, c=c):
                at = (3 * c + 1) * tt
                gs2[hd, i] = gacc[hd, at : at + tt, :].astype(BF16)
                back2(hd, side).start()
            pl.when(there[side])(send)

    out_cols = slice(3 * width, 4 * width)
    own_mixed = mm(att[...], W[own_rows, out_cols], NT)
    if gather:
        def weights_in(i):
            yv(i).wait_recv()
            yv(i).wait_send()
            yc(i).wait_send()

        for i in range(total):
            pl.when(held(i))(functools.partial(weights_in, i))
    else:
        w_copy.wait_recv()
    for hd in range(heads):
        to_peer(0, hd).wait_recv()
    mixed[...] = (own_mixed + mm(atto[...], Wo[:, out_cols], NT)).astype(BF16)

    total_in = mm(gqkv[:, 0:width], W[own_rows, 0:width], NT)
    for hd in range(heads):
        to_peer(1, hd).wait_recv()
    total_in += mm(gqkvo[:, 0:width], Wo[:, 0:width], NT)

    for hd in range(heads):
        for i, (side, other, c) in enumerate((("l", "r", 1), ("r", "l", 2))):
            def add2(i=i, other=other, c=c):
                back2(hd, other).wait_recv()
                at = (3 * c + 1) * tt
                gacc[hd, at : at + tt, :] += gr2[hd, 1 - i].astype(F32)
            pl.when(there[side])(add2)
        cols = slice(hd * HEAD_DIM, (hd + 1) * HEAD_DIM)
        kcols = slice(width + hd * HEAD_DIM, width + (hd + 1) * HEAD_DIM)
        vcols = slice(2 * width + hd * HEAD_DIM, 2 * width + (hd + 1) * HEAD_DIM)
        for j in range(2):
            rows_j = slice(j * tt, (j + 1) * tt)
            at = (3 * (1 + j) + 1) * tt
            gqkv[rows_j, kcols] = norm_back(
                raw[rows_j, kcols], kg[:, cols], gacc[hd, at : at + tt, 0:HEAD_DIM])
            gqkv[rows_j, vcols] = gacc[hd, at : at + tt, HEAD_DIM:].astype(BF16)
        to_peer(2, hd).start()
        to_peer(3, hd).start()

    total_in += mm(gqkv[:, width:], W[own_rows, width : 3 * width], NT)
    for hd in range(heads - 1):
        to_peer(2, hd).wait_recv()
        to_peer(3, hd).wait_recv()
    early = (slice(width, 2 * width - HEAD_DIM), slice(2 * width, 3 * width - HEAD_DIM))
    late = (slice(2 * width - HEAD_DIM, 2 * width), slice(3 * width - HEAD_DIM, 3 * width))
    for part in early:
        total_in += mm(gqkvo[:, part], Wo[:, part], NT)
    to_peer(2, heads - 1).wait_recv()
    to_peer(3, heads - 1).wait_recv()
    for part in late:
        total_in += mm(gqkvo[:, part], Wo[:, part], NT)
    gin[...] = total_in.astype(BF16)

    if gather:
        all_sent()
    else:
        w_copy.wait_send()
    for hd in range(heads):
        for part in range(4):
            to_peer(part, hd).wait_send()
        for side in "lrud":
            pl.when(there[side])(lambda: side_copy(hd, side).wait_send())
        for s in "ud":
            pl.when(there[s] & left)(lambda: corner(hd, s, 0).wait_send())
            pl.when(there[s] & right)(lambda: corner(hd, s, 3).wait_send())
            pl.when(there[s])(lambda: back(hd, s).wait_send())
        for s in "lr":
            pl.when(there[s])(lambda: back2(hd, s).wait_send())


def on_device(nh, nw, tokens, grad_out, qkv_weight, out_weight, q_gain, k_gain, key_valid):
    tile_rows, tile_cols, tt, model = tokens.shape
    count = tile_rows * tile_cols * tt
    width = q_gain.shape[0]
    heads = width // HEAD_DIM
    weights = [qkv_weight.reshape(qkv_weight.shape[0], 3 * width), out_weight]
    gather = nh == 4 and nw > 1 and out_weight.shape[0] % 32 == 0
    if not gather:
        whole = jnp.concatenate(weights, axis=1)
        weights = [lax.all_gather(whole, ("height", "width"), axis=0, tiled=True)]
    vcol = jnp.broadcast_to(key_valid.astype(F32).reshape(count, 1), (count, HEAD_DIM))
    half = model // 2
    vm = pltpu.VMEM
    dma = pltpu.SemaphoreType.DMA
    scratch = [vm((model, 4 * width), BF16)] if gather else []
    scratch += [
        vm((count, 3 * width), F32),
        vm((count, width), BF16),
        vm((count, width), BF16),
        vm((heads, 4, 3, tt, 2 * HEAD_DIM), BF16),
        vm((12 * tt, 2 * HEAD_DIM), BF16),
        vm((heads, 12 * tt, 2 * HEAD_DIM), F32),
        vm((count, width), BF16),
        vm((count, width), F32),
        vm((heads, 2, 4, tt, 2 * HEAD_DIM), BF16),
        vm((heads, 2, 4, tt, 2 * HEAD_DIM), BF16),
        vm((heads, 2, tt, 2 * HEAD_DIM), BF16),
        vm((heads, 2, tt, 2 * HEAD_DIM), BF16),
        vm((count, 3 * width), BF16),
        vm((count, width), BF16),
        vm((count, 3 * width), BF16),
        vm((half, 4 * width), BF16),
        vm((count, model), BF16),
        vm((count, model), BF16),
        dma((heads, 8)), dma((heads, 8)),
        dma((heads, 4)), dma((heads, 4)),
        dma((4 * heads,)), dma((4 * heads,)),
        dma((2 * nw - 1,)), dma((2 * nw - 1,)),
        dma((2,)),
    ]
    if gather:
        n = 2 * nw - 1
        scratch += [dma((2, nw - 1)), dma((2, nw - 1)), dma((n,)), dma((n,)),
                    dma((2 * n,)), dma((2 * n,)), dma((n,)), dma((n,))]
    mixed, grad_in = pl.pallas_call(
        functools.partial(body, (nh, nw, heads, tt, gather)),
        out_shape=[jax.ShapeDtypeStruct((count, half), BF16)] * 2,
        in_specs=[pl.BlockSpec(memory_space=pl.ANY)] * 2
        + [pl.BlockSpec(memory_space=pltpu.VMEM)] * (3 + len(weights)),
        out_specs=[pl.BlockSpec(memory_space=pltpu.VMEM)] * 2,
        scratch_shapes=scratch,
        compiler_params=pltpu.CompilerParams(
            collective_id=0, has_side_effects=True, vmem_limit_bytes=56 * 1024 * 1024),
    )(tokens.reshape(count, model), grad_out.reshape(count, model),
      q_gain, k_gain, vcol, *weights)
    shape = (tile_rows, tile_cols, tt, half)
    return mixed.reshape(shape), grad_in.reshape(shape)


def solution(mesh):
    placed = (
        P("height", "width", None, None),
        P("height", "width", None, None),
        P(("height", "width"), None, "head"),
        P(("height", "width"), "head"),
        P("head"),
        P("head"),
        P("height", "width", None),
    )
    return jax.shard_map(
        functools.partial(on_device, mesh.shape["height"], mesh.shape["width"]),
        mesh=mesh,
        in_specs=placed,
        out_specs=(P("height", "width", None, "head"), P("height", "width", None, "head")),
        check_vma=False,
    )
```
